128 devices in a mesh: grp: 4 (over z), dev: 32 (over x, y, core).
Axes of the slice: x: 4, y: 4, z: 4, core: 2. Of those that a mesh axis runs over, the one named last changes fastest.
Arguments:
- head_emb: bfloat16 [131072, 400], P(('grp', 'dev')), may hold values from -2 to 2
- tail_emb: bfloat16 [131072, 400], P(('grp', 'dev')), may hold values from -2 to 2
- relation: int32 [131072], P(('grp', 'dev')), may hold values from 0 to 14823
- owners: int32 [131072, 2], P(('grp', 'dev')), may hold values from 0 to 127, all different within a row; in each aligned block of 1024 rows (0 to 1023, 1024 to 2047, ...) at most 32 rows name the same one
- owner_rows: int32 [131072, 2], P(('grp', 'dev')), may hold values from 0 to 4095
- entities: bfloat16 [524288, 400], P(('grp', 'dev')), may hold values from -2 to 2
- neg_rows: int32 [1, 16384], P(None, ('grp', 'dev')), may hold values from 0 to 4095
- coef: float32 [14824, 100], replicated, may hold values from -4 to 4
- bases: float32 [100, 400], replicated, may hold values from -0.625 to 0.625
Outputs:
- ent_grad: float32 [524288, 400], P(('grp', 'dev'))
- coef_grad: float32 [14824, 100], replicated
- bases_grad: float32 [100, 400], replicated
The draws below stay inside these ranges and needn't reach their ends.
Inputs may be any that keep to these rules, and one draw needn't show every extreme that they name: The two owners of a row differ; within the triples of one device no owner is named by more than 32 entries of both columns together.
All inputs are finite; a program needn't handle non-finite values.
Results may differ from the reference program's by a relative error of at most 0.0029.
Values may be sent and summed in bfloat16 or wider, within the bound.
A program may use at most 128 MiB of HBM per device.

```python
import math
import jax
import jax.numpy as jnp
import numpy as np
from jax import lax

D = 400
NREL = 14824
NB = 100
BLOCK = 1024
TRIP_DEV = 1024
NEG_DEV = 128
ENT_DEV = 4096
BLOCKS = 1
CAP = 32
TRIPLES = 131072
NENT = 524288
N_GRP = 4
N_DEV = 32
DEVICES = 128


def touch_ends(entries, key, low, top_value):
    spot = [jax.random.randint(jax.random.fold_in(key, axis), (), 0, length) for axis, length in enumerate(entries.shape)]
    widest = entries.shape.index(max(entries.shape))
    beside = spot[:widest] + [(spot[widest] + 1) % entries.shape[widest]] + spot[widest + 1:]
    return entries.at[tuple(spot)].set(low).at[tuple(beside)].set(top_value)


def levels(rng, dims, split, smallest, largest):
    level = 1.0
    for axis_at, parts in split:
        heights = jax.random.uniform(jax.random.fold_in(jax.random.fold_in(rng, 6), axis_at), (parts,), jnp.float32, smallest / len(split), largest / len(split))
        level = level * jnp.repeat(jnp.exp(heights), dims[axis_at] // parts).reshape((-1,) + (1,) * (len(dims) - 1 - axis_at))
    return level


def rank_bounds(count, lean):
    portions = [(1 << 20) // math.isqrt(rank ** lean) + 1 for rank in range(1, count + 1)]
    spread = 1 + sum(portions) // (1 << 30)
    return np.cumsum(np.array([max(1, weight // spread) for weight in portions]))


def ranked_ids(stream_key, extent, amount, skew):
    grid = rank_bounds(amount, skew)
    ticket = jax.random.randint(jax.random.fold_in(stream_key, 1), extent, 0, int(grid[amount - 1]))
    rank = jnp.searchsorted(jnp.asarray(grid, jnp.int32), ticket, side="right")
    return jax.random.permutation(jax.random.fold_in(stream_key, 2), amount)[rank].astype(jnp.int32)


def deal_out(stream_key, own, number, rows, count, top, reach, slope):
    sequence = jax.random.permutation(stream_key, count)
    crowded, ordinary = shares(count, rows * top, reach, slope, True), shares(count, rows * top, reach, slope, False)
    places = jnp.arange(count)

    def named(tallies, turn):
        used = int((tallies > 0).sum())
        fixed = max(1, used // 4)
        shifted = fixed + (places - fixed + turn * (used - fixed)) % max(1, count - fixed)
        return jnp.zeros((count,), jnp.int32).at[sequence[jnp.where(places < fixed, places, shifted)]].set(jnp.asarray(tallies, jnp.int32))

    tallies = jnp.where(number % 4 == 0, named(crowded, number // 4), named(ordinary, number - number // 4 - 1))
    mixed = jax.random.permutation(jax.random.fold_in(own, 3), count)
    giver, taker = mixed[0:count // 2 * 2:2], mixed[1:count // 2 * 2:2]
    margin = jnp.minimum(tallies[giver] - 1, reach - tallies[taker]) // 2
    margin = jnp.where((giver == sequence[0]) | (taker == sequence[0]) | (tallies[taker] == 0), 0, jnp.maximum(margin, 0))
    shifted = jax.random.randint(jax.random.fold_in(own, 4), (count // 2,), 0, 1 << 20) % (margin + 1)
    tallies = tallies.at[giver].add(-shifted).at[taker].add(shifted)
    items = jnp.searchsorted(jnp.cumsum(tallies), jnp.arange(rows * top), side="right").astype(jnp.int32)
    listing = items.reshape(top, rows).T
    listing = listing[jax.random.permutation(jax.random.fold_in(own, 1), rows)]
    turn = jax.random.randint(jax.random.fold_in(own, 2), (rows, 1), 0, top)
    return jnp.take_along_axis(listing, (jnp.arange(top)[None, :] + turn) % top, axis=1)


def shares(amount, total, reach, skew, full):
    portions = [(1 << 20) // math.isqrt(grade ** skew) + 1 for grade in range(1, amount + 1)]
    largest = reach if full else min(reach, max(-(-total // amount), total * portions[0] // sum(portions)))
    least = 1 if total - largest >= amount - 1 else 0
    given, spare = [largest] + [least] * (amount - 1), total - largest - least * (amount - 1)
    while spare > 0:
        candidates = [i for i in range(1, amount) if given[i] < largest] or [i for i in range(1, amount) if given[i] < reach]
        whole, remaining = sum([portions[i] for i in candidates]), spare
        for i in candidates:
            addition = min(reach - given[i], max(1, remaining * portions[i] // whole), spare)
            given[i] = given[i] + addition
            spare = spare - addition
    return np.array(given)


def scatter_about(key, shape, scale, bound, split=(), kind=jnp.bfloat16):
    array = scale * jax.random.normal(key, shape, jnp.float32)
    if split:
        array = array * levels(key, shape, split, -0.22, 0.18)
    return jnp.clip(array, -bound, bound).astype(kind)


def setup_inputs(seed: int = 0) -> dict:
    key_of = jax.random.split(jax.random.key(seed), 10)
    head_emb = scatter_about(key_of[0], (TRIPLES, D), 0.3, 2.0, ((0, 128),))
    tail_emb = scatter_about(key_of[1], (TRIPLES, D), 0.3, 2.0, ((0, 128),))
    relation = touch_ends(ranked_ids(key_of[2], (TRIPLES,), NREL, 2), jax.random.fold_in(key_of[2], 3), 0, NREL - 1).astype(jnp.int32)
    owners_keys = jax.random.split(jax.random.fold_in(key_of[3], 1), TRIPLES // TRIP_DEV)
    owners_turns = jax.random.permutation(jax.random.fold_in(key_of[3], 3), TRIPLES // TRIP_DEV)
    owners = jax.vmap(lambda own, number: deal_out(jax.random.fold_in(key_of[3], 2), own, number, TRIP_DEV, DEVICES, 2, CAP, 2))(owners_keys, owners_turns).reshape((TRIPLES, 2))
    owner_rows = touch_ends(jax.random.randint(key_of[4], (TRIPLES, 2), 0, ENT_DEV), jax.random.fold_in(key_of[4], 1), 0, ENT_DEV - 1).astype(jnp.int32)
    entities = scatter_about(key_of[5], (NENT, D), 0.3, 2.0, ((0, 128),))
    neg_rows = touch_ends(jax.random.randint(key_of[6], (BLOCKS, NEG_DEV * DEVICES), 0, ENT_DEV), jax.random.fold_in(key_of[6], 1), 0, ENT_DEV - 1).astype(jnp.int32)
    coef = scatter_about(key_of[7], (NREL, NB), 1.0, 4.0, (), jnp.float32)
    bases = scatter_about(key_of[8], (NB, D), NB ** -0.5, 0.625, (), jnp.float32)
    return dict(head_emb=head_emb, tail_emb=tail_emb, relation=relation, owners=owners, owner_rows=owner_rows, entities=entities, neg_rows=neg_rows, coef=coef, bases=bases)


def score_block(packed, entities, coef, bases):
    head_blk, tail_blk, rel_blk, neg_ids = packed
    highest = lax.Precision.HIGHEST
    neg_count = NEG_DEV * N_DEV
    picked = coef[rel_blk]
    rel_vec = jnp.dot(picked, bases, precision=highest)
    negatives = entities[neg_ids]
    head_f = head_blk.astype(jnp.float32)
    tail_f = tail_blk.astype(jnp.float32)
    head_rel = (head_f * rel_vec).astype(jnp.bfloat16)
    neg_prob = jax.nn.sigmoid(jnp.dot(head_rel, negatives.T, preferred_element_type=jnp.float32)).astype(jnp.bfloat16)
    neg_mix = jnp.dot(neg_prob, negatives, preferred_element_type=jnp.float32)
    neg_grad = jnp.dot(neg_prob.T, head_rel, preferred_element_type=jnp.float32) / neg_count
    pos_gate = jax.nn.sigmoid(-jnp.sum(head_f * rel_vec * tail_f, axis=1))[:, None]
    head_grad = (-pos_gate * rel_vec * tail_f + rel_vec * neg_mix / neg_count).astype(jnp.bfloat16)
    tail_grad = (-pos_gate * head_f * rel_vec).astype(jnp.bfloat16)
    rel_grad = -pos_gate * head_f * tail_f + head_f * neg_mix / neg_count
    coef_rows = jnp.dot(rel_grad, bases.T, precision=highest)
    bases_part = jnp.dot(picked.T, rel_grad, precision=highest)
    return head_grad, tail_grad, neg_grad, coef_rows, bases_part


def reference(head_emb, tail_emb, relation, owners, owner_rows, entities, neg_rows, coef, bases):
    all_devices = N_GRP * N_DEV
    neg_count = NEG_DEV * N_DEV
    block_count = TRIP_DEV // BLOCK
    source_dev = (jnp.arange(all_devices * NEG_DEV) // NEG_DEV).astype(jnp.int32)
    neg_ids = (source_dev[None, :] * ENT_DEV + neg_rows).astype(jnp.int32)
    neg_ids = neg_ids.reshape(block_count, N_GRP, neg_count).transpose(1, 0, 2).reshape(N_GRP * block_count, neg_count)

    def arrange(values):
        tail_shape = values.shape[1:]
        shaped = values.reshape((N_GRP, N_DEV, block_count, BLOCK) + tail_shape)
        order = (0, 2, 1, 3) + tuple(range(4, 4 + len(tail_shape)))
        return shaped.transpose(order).reshape((N_GRP * block_count, N_DEV * BLOCK) + tail_shape)

    def restore(values):
        tail_shape = values.shape[2:]
        shaped = values.reshape((N_GRP, block_count, N_DEV, BLOCK) + tail_shape)
        order = (0, 2, 1, 3) + tuple(range(4, 4 + len(tail_shape)))
        return shaped.transpose(order).reshape((N_GRP * N_DEV * TRIP_DEV,) + tail_shape)

    rel_arranged = arrange(relation)
    packed = (arrange(head_emb), arrange(tail_emb), rel_arranged, neg_ids)
    head_grad, tail_grad, neg_grad, coef_rows, bases_part = lax.map(
        lambda item: score_block(item, entities, coef, bases), packed)
    head_grad = restore(head_grad)
    tail_grad = restore(tail_grad)
    target = (owners * ENT_DEV + owner_rows).astype(jnp.int32).reshape(-1)
    grad_rows = jnp.stack([head_grad, tail_grad], axis=1).astype(jnp.float32).reshape(-1, D)
    ent_grad = jnp.zeros((N_GRP * N_DEV * ENT_DEV, D), jnp.float32)
    ent_grad = ent_grad.at[target].add(grad_rows)
    ent_grad = ent_grad.at[neg_ids.reshape(-1)].add(neg_grad.reshape(-1, D))
    coef_grad = jax.ops.segment_sum(coef_rows.reshape(-1, NB), rel_arranged.reshape(-1), num_segments=NREL)
    bases_grad = jnp.sum(bases_part, axis=0)
    return ent_grad, coef_grad, bases_grad
```

```python
import functools

import jax
import jax.numpy as jnp
from jax import lax
from jax.experimental import pallas as pl
from jax.experimental.pallas import tpu as pltpu
from jax.sharding import PartitionSpec as P

MESH = pl.DeviceIdType.MESH
HIGHEST = lax.Precision.HIGHEST
D = 400
NB = 100
TRIP = 1024
NEG = 128
ENT = 4096
NREL = 14824
GROUP = 32
NEG_ALL = NEG * GROUP
RA = (0, 208)
RB = (208, 192)
LOROW = 112
VM = pl.BlockSpec(memory_space=pltpu.VMEM)
ANY = pl.BlockSpec(memory_space=pl.ANY)
BF = jnp.bfloat16
F32 = jnp.float32


def dot(a, b, ca=1, cb=0, precision=None):
    return lax.dot_general(
        a, b, (((ca,), (cb,)), ((), ())), preferred_element_type=F32, precision=precision
    )


def spread(ids, rows):
    return (lax.broadcasted_iota(jnp.int32, (rows, ids.shape[1]), 0) == ids).astype(F32).astype(BF)


def equals(ids, value):
    return (ids == value).astype(F32).astype(BF)


def score_kernel(
    head, tail, rel, owners, negr, basest, coeft, entt,
    own_neg, grads, rows, bases_part, pos,
    coefv, entv, st, oh, pk, picked, relv, hrt, hr, mix, got, grd, pair, r2a, r2b, s3a, s3b, r3, blk,
    ss, rs, loc,
):
    g, k = lax.axis_index("grp"), lax.axis_index("dev")
    x, y, c = k // 8, lax.rem(k // 2, 4), lax.rem(k, 2)

    def dev(dx, dy, dc):
        return (g, (lax.rem(x + dx, 4) * 4 + lax.rem(y + dy, 4)) * 2 + lax.rem(c + dc, 2))

    get_ent = pltpu.make_async_copy(entt, entv, loc.at[0])
    get_ent.start()
    get_coef = pltpu.make_async_copy(coeft, coefv, loc.at[1])
    get_coef.start()
    bar = pltpu.get_barrier_semaphore()
    XP = [dev(d, 0, 0) for d in (1, 2, 3)]
    YP = [dev(0, d, 0) for d in (1, 2, 3)]
    CP = dev(0, 0, 1)
    for p in XP + YP + [CP]:
        pl.semaphore_signal(bar, inc=1, device_id=p, device_id_type=MESH)
    count = [0]
    sent = []

    def send(src, dst, p):
        i = count[0]
        count[0] += 1
        cp = pltpu.make_async_remote_copy(
            src_ref=src, dst_ref=dst, send_sem=ss.at[i], recv_sem=rs.at[i], device_id=p, device_id_type=MESH
        )
        cp.start()
        sent.append(cp)
        return cp

    pick_neg = spread(negr[...], ENT)
    get_ent.wait()
    got[c, y, x] = dot(entv[...], pick_neg).astype(BF)
    pl.semaphore_wait(bar, 7)
    A, B = pl.ds(*RA), pl.ds(*RB)
    mine_a, mine_b = got.at[c, y, x, A], got.at[c, y, x, B]
    a1 = [send(mine_a, mine_a, XP[d]) for d in (1, 0, 2)]
    b1 = [send(mine_b, mine_b, YP[d]) for d in (1, 0, 2)]

    st[...] = jnp.zeros_like(st)
    pk[...] = jnp.zeros_like(pk)
    ids = rel[...]
    low = spread(ids & 255, 256)
    high = lax.shift_right_logical(ids, 8)
    get_coef.wait()

    def load_coef(base, width, at):
        part = coefv[:, pl.ds(base, width)]
        first = part.astype(BF)
        st[0:NB, at : at + width] = first
        st[LOROW : LOROW + NB, at : at + width] = (part - first.astype(F32)).astype(BF)

    def gather(step):
        base = pl.multiple_of(step * 1024, 1024)
        load_coef(base, 1024, 0)
        for q in range(4):
            oh[q * 256 : (q + 1) * 256, :] = low * equals(high, step * 4 + q)
        pk[...] += dot(st[...], oh[...])

    def gather_loop(start, stop):
        def body(i, carry):
            gather(i)
            return carry

        lax.fori_loop(start, stop, body, 0)

    gather_loop(0, 5)
    for cp in a1:
        cp.wait_recv()
    line_a = got.at[c, y, :, A]
    a2 = [send(line_a, line_a, YP[d]) for d in (1, 0, 2)]
    for cp in b1:
        cp.wait_recv()
    line_b = got.at[c, :, x, B]
    b2 = [send(line_b, line_b, XP[d]) for d in (1, 0, 2)]
    last = [send(line_a, line_a, CP), send(line_b, line_b, CP)]

    gather_loop(5, 14)
    full = NREL // 1024 * 1024
    rest = NREL - full - 256
    load_coef(full, 256, 0)
    load_coef(full + 256, rest, 256)
    for q in range(2):
        oh[q * 256 : (q + 1) * 256, :] = low * equals(high, full // 256 + q)
    pk[...] += dot(st[:, 0 : 256 + rest], oh[0 : 256 + rest, :])
    chosen = pk[0:NB] + pk[LOROW : LOROW + NB]
    picked[...] = chosen
    relv[...] = dot(basest[...], chosen, precision=HIGHEST)
    hb = (head[...].astype(F32) * relv[...]).astype(BF)
    hrt[...] = hb
    hr[...] = hb.T
    tri = (
        lax.broadcasted_iota(jnp.int32, (256, 256), 0) < lax.broadcasted_iota(jnp.int32, (256, 256), 1)
    ).astype(F32).astype(BF)
    before = jnp.zeros((128, 1), F32)
    for h in range(2):
        for b in range(4):
            o = owners[h : h + 1, b * 256 : (b + 1) * 256]
            one = spread(o, 128)
            onef = one.astype(F32)
            rank = jnp.sum((dot(one, tri) + before) * onef, axis=0, keepdims=True)
            before = before + jnp.sum(onef, axis=1, keepdims=True)
            pos[h : h + 1, b * 256 : (b + 1) * 256] = o * 32 + rank.astype(jnp.int32)

    for j, d in ((1, 1), (2, 3), (0, 2)):
        a2[j].wait_recv()
        r = got.at[c, lax.rem(y - d + 4, 4), :, A]
        last.append(send(r, r, CP))
        b2[j].wait_recv()
        r = got.at[c, :, lax.rem(x - d + 4, 4), B]
        last.append(send(r, r, CP))
    for cp in last:
        cp.wait_recv()

    mix[...] = jnp.zeros_like(mix)

    def chunk(cc, yy):
        for q in range(4):
            blk[:, q * 128 : (q + 1) * 128] = got[cc, yy, q]
        n = blk[...]
        s = dot(hr[...], n)
        prob = (0.5 * jnp.tanh(0.5 * s) + 0.5).astype(BF)
        mix[...] += dot(n, prob, 1, 1)
        part = (dot(hrt[...], prob) * (1.0 / NEG_ALL)).astype(BF)
        for q in range(4):
            grd[cc, yy, q] = part[:, q * 128 : (q + 1) * 128]

    halves = []
    for s in range(4):
        yy = lax.rem(y + 1 + s, 4)
        chunk(1 - c, yy)
        halves.append(send(grd.at[1 - c, yy], pair.at[yy], CP))
    a4, b4 = [], []
    for s in range(4):
        yy = lax.rem(y + 1 + s, 4)
        chunk(c, yy)
        halves[s].wait_recv()
        grd[c, yy] = (grd[c, yy].astype(F32) + pair[yy].astype(F32)).astype(BF)
        if s < 3:
            a4.append(send(grd.at[c, yy, :, A], r2a.at[s], YP[s]))
        for d in (1, 2, 3):
            xx = lax.rem(x + d, 4)
            b4.append(send(grd.at[c, yy, xx, B], r2b.at[d - 1, yy], XP[d - 1]))

    h, t = head[...].astype(F32), tail[...].astype(F32)
    rv = relv[...]
    hrv = h * rv
    score = jnp.sum(hrv * t, axis=0, keepdims=True)
    gate = 0.5 - 0.5 * jnp.tanh(0.5 * score)
    mean = mix[...] * (1.0 / NEG_ALL)
    inner = mean - gate * t
    grads[0] = (rv * inner).astype(BF)
    grads[1] = (-gate * hrv).astype(BF)
    rg = h * inner

    for cp in a4:
        cp.wait_recv()
    tot = grd[c, y, :, 0:208, :].astype(F32)
    for d in range(3):
        tot += r2a[d].astype(F32)
    s3a[...] = tot.astype(BF)
    a5 = [send(s3a.at[lax.rem(x + d, 4)], r3.at[d - 1, A], XP[d - 1]) for d in (1, 2, 3)]
    for cp in b4:
        cp.wait_recv()
    tot = grd[c, :, x, 208:400, :].astype(F32)
    for d in range(3):
        tot += r2b[d].astype(F32)
    s3b[...] = tot.astype(BF)
    b5 = [send(s3b.at[lax.rem(y + d, 4)], r3.at[d - 1, B], YP[d - 1]) for d in (1, 2, 3)]

    crow = dot(basest[...], rg, 0, 0, precision=HIGHEST)
    first = crow.astype(BF)
    rows[...] = jnp.zeros_like(rows)
    rows[0:NB] = first
    rows[LOROW : LOROW + NB] = (crow - first.astype(F32)).astype(BF)
    bases_part[...] = jnp.zeros_like(bases_part)
    bases_part[0:D, 0:NB] = dot(rg, picked[...], 1, 1, precision=HIGHEST)

    for cp in a5:
        cp.wait_recv()
    tot = s3a[x].astype(F32)
    for d in range(3):
        tot += r3[d, 0:208].astype(F32)
    own_neg[0:208] = tot
    for cp in b5:
        cp.wait_recv()
    tot = s3b[y].astype(F32)
    for d in range(3):
        tot += r3[d, 208:400].astype(F32)
    own_neg[208:400] = tot
    for cp in sent:
        cp.wait_send()


def score(head, tail, rel, owners, negr, basest, coeft, entt):
    sem = pltpu.SemaphoreType.DMA
    v = pltpu.VMEM
    return pl.pallas_call(
        score_kernel,
        out_shape=(
            jax.ShapeDtypeStruct((D, NEG), F32),
            jax.ShapeDtypeStruct((2, D, TRIP), BF),
            jax.ShapeDtypeStruct((224, TRIP), BF),
            jax.ShapeDtypeStruct((448, 128), F32),
            jax.ShapeDtypeStruct((2, TRIP), jnp.int32),
        ),
        in_specs=[VM] * 6 + [ANY] * 2,
        out_specs=(VM,) * 5,
        scratch_shapes=[
            v((NB, NREL), F32), v((D, ENT), BF), v((224, 1024), BF), v((1024, TRIP), BF), v((224, TRIP), F32),
            v((NB, TRIP), F32), v((D, TRIP), F32), v((D, TRIP), BF), v((TRIP, D), BF), v((D, TRIP), F32),
            v((2, 4, 4, D, NEG), BF), v((2, 4, 4, D, NEG), BF), v((4, 4, D, NEG), BF),
            v((3, 4, 208, NEG), BF), v((3, 4, 192, NEG), BF), v((4, 208, NEG), BF), v((4, 192, NEG), BF),
            v((3, D, NEG), BF), v((D, 512), BF),
            sem((48,)), sem((48,)), sem((2,)),
        ],
        compiler_params=pltpu.CompilerParams(collective_id=0, has_side_effects=True, vmem_limit_bytes=56 * 2**20),
        cost_estimate=pl.CostEstimate(flops=10**11, bytes_accessed=10**7, transcendentals=4 * 10**6),
        name="score",
    )(head, tail, rel, owners, negr, basest, coeft, entt)


def pack_kernel(pos, orow, grads, out, gn, low):
    step = pl.program_id(0)

    @pl.when(step == 0)
    def _():
        for h in range(2):
            at = h * TRIP
            low[:, at : at + TRIP] = spread(pos[h : h + 1] & 255, 256)
            r = orow[h : h + 1].astype(jnp.int32)
            two = lax.broadcasted_iota(jnp.int32, (112, TRIP), 0)
            extra = jnp.where(two == 0, lax.shift_right_logical(r, 6), jnp.where(two == 1, r & 63, 0))
            g = jnp.concatenate([grads[h], extra.astype(F32).astype(BF)], axis=0)
            gn[at : at + TRIP, :] = g.T

    tot = None
    for h in range(2):
        at = h * TRIP
        one = low[:, at : at + TRIP] * equals(lax.shift_right_logical(pos[h : h + 1], 8), step)
        d = dot(one, gn[at : at + TRIP])
        tot = d if tot is None else tot + d
    out[...] = tot.astype(BF)


def pack(pos, orow, grads):
    whole = lambda *s: pl.BlockSpec(s, lambda i: (0,) * len(s))
    return pl.pallas_call(
        pack_kernel,
        grid=(16,),
        out_shape=jax.ShapeDtypeStruct((4096, 512), BF),
        in_specs=[whole(2, TRIP), whole(2, TRIP), whole(2, D, TRIP)],
        out_specs=pl.BlockSpec((256, 512), lambda i: (i, 0)),
        scratch_shapes=[pltpu.VMEM((2 * TRIP, 512), BF), pltpu.VMEM((256, 2 * TRIP), BF)],
        compiler_params=pltpu.CompilerParams(vmem_limit_bytes=40 * 2**20),
        cost_estimate=pl.CostEstimate(flops=9 * 10**9, bytes_accessed=6 * 10**6, transcendentals=0),
        name="pack",
    )(pos, orow, grads)


WIDE = 4096 + 2 * NEG


def place_kernel(recv, own_neg, negr, out, rt, low, ids):
    step = pl.program_id(0)

    @pl.when(step == 0)
    def _():
        for q in range(8):
            at = q * 512
            rt[:, at : at + 512] = recv[at : at + 512, :].T
            a = rt[400:416, at : at + 512].astype(F32)
            ids[:, at : at + 512] = (a[0:1] * 64.0 + a[1:2]).astype(jnp.int32)
        n = own_neg[...]
        first = n.astype(BF)
        rt[0:D, 4096 : 4096 + NEG] = first
        rt[0:D, 4096 + NEG : WIDE] = (n - first.astype(F32)).astype(BF)
        ids[:, 4096 : 4096 + NEG] = negr[...]
        ids[:, 4096 + NEG : WIDE] = negr[...]
        low[...] = spread(ids[...] & 255, 256)

    one = low[...] * equals(lax.shift_right_logical(ids[...], 8), step)
    out[...] = dot(rt[0:D, :], one, 1, 1)


def place(recv, own_neg, negr):
    whole = lambda *s: pl.BlockSpec(s, lambda i: (0,) * len(s))
    return pl.pallas_call(
        place_kernel,
        grid=(16,),
        out_shape=jax.ShapeDtypeStruct((D, ENT), F32),
        in_specs=[whole(4096, 512), whole(D, NEG), whole(1, NEG)],
        out_specs=pl.BlockSpec((D, 256), lambda i: (0, i)),
        scratch_shapes=[pltpu.VMEM((512, WIDE), BF), pltpu.VMEM((256, WIDE), BF), pltpu.VMEM((1, WIDE), jnp.int32)],
        compiler_params=pltpu.CompilerParams(vmem_limit_bytes=40 * 2**20),
        cost_estimate=pl.CostEstimate(flops=14 * 10**9, bytes_accessed=11 * 10**6, transcendentals=0),
        name="place",
    )(recv, own_neg, negr)


RANGE = 1920


def reduce_kernel(
    rows, rel, bpart, out,
    gr, gi, gb, acc, rsb, r2a, r2b, s3a, s3b, r3, ss, rs, loc,
):
    z, k = lax.axis_index("grp"), lax.axis_index("dev")
    x, y, c = k // 8, lax.rem(k // 2, 4), lax.rem(k, 2)
    own = z * 2 + c

    def dev(dx, dy, dz, dc):
        return (lax.rem(z + dz, 4), (lax.rem(x + dx, 4) * 4 + lax.rem(y + dy, 4)) * 2 + lax.rem(c + dc, 2))

    XP = [dev(d, 0, 0, 0) for d in (1, 2, 3)]
    YP = [dev(0, d, 0, 0) for d in (1, 2, 3)]
    ZP = [dev(0, 0, d, 0) for d in (1, 2, 3)]
    ZC = [dev(0, 0, d, 1) for d in (1, 2, 3)]
    CP = dev(0, 0, 0, 1)
    bar = pltpu.get_barrier_semaphore()
    for p in XP + YP + ZP + ZC + [CP]:
        pl.semaphore_signal(bar, inc=1, device_id=p, device_id_type=MESH)
    keep = [
        pltpu.make_async_copy(rows, gr.at[own], loc.at[0]),
        pltpu.make_async_copy(rel, gi.at[own], loc.at[1]),
        pltpu.make_async_copy(bpart.at[pl.ds(pl.multiple_of(own * 56, 8), 56)], gb.at[own], loc.at[2]),
    ]
    for cp in keep:
        cp.start()
    count = [0]
    sent = []

    def send(src, dst, p):
        i = count[0]
        count[0] += 1
        cp = pltpu.make_async_remote_copy(
            src_ref=src, dst_ref=dst, send_sem=ss.at[i], recv_sem=rs.at[i], device_id=p, device_id_type=MESH
        )
        cp.start()
        sent.append(cp)
        return cp

    for cp in keep:
        cp.wait()
    pl.semaphore_wait(bar, 13)
    first = [
        [send(rel, gi.at[own], ZP[d]), send(rows, gr.at[own], ZP[d])] for d in (0, 2, 1)
    ]
    near = [send(rel, gi.at[own], CP), send(rows, gr.at[own], CP)]
    pieces = []

    def piece(dz, dc, p):
        r = lax.rem(z + dz, 4) * 2 + lax.rem(c + dc, 2)
        pieces.append(send(bpart.at[pl.ds(pl.multiple_of(r * 56, 8), 56)], gb.at[own], p))

    piece(0, 1, CP)
    for d in (1, 2, 3):
        piece(d, 0, ZP[d - 1])
        piece(d, 1, ZC[d - 1])

    def add(j, start):
        ids = gi[j] - own * RANGE
        low = spread(ids & 255, 256)
        high = lax.shift_right_arithmetic(ids, 8)
        r = gr[j]
        for t in range(8):
            p = dot(r * equals(high, t), low, 1, 1)
            p = p[0:104] + p[LOROW : LOROW + 104]
            if start:
                acc[t] = p
            else:
                acc[t] += p

    add(own, True)
    for cp in near:
        cp.wait_recv()
    add(z * 2 + 1 - c, False)
    more = []
    for i, d in enumerate((1, 3, 2)):
        src = lax.rem(z - d + 4, 4) * 2
        for cp in first[i]:
            cp.wait_recv()
        more = [send(gi.at[src + c], gi.at[src + c], CP), send(gr.at[src + c], gr.at[src + c], CP)]
        add(src + c, False)
        for cp in more:
            cp.wait_recv()
        add(src + 1 - c, False)
    for cp in pieces:
        cp.wait_recv()
    tot = gb[0]
    for j in range(1, 8):
        tot += gb[j]
    for q in range(16):
        if q == 15:
            rsb[3, 3] = jnp.zeros((104, 128), F32)
            rsb[3, 3, 0:56] = tot
        else:
            rsb[q // 4, q % 4] = acc[q // 2, :, (q % 2) * 128 : (q % 2) * 128 + 128]
    A, B = pl.ds(0, 56), pl.ds(56, 48)
    a4, b4 = [], []
    for d in (2, 1, 3):
        yy, xx = lax.rem(y + d, 4), lax.rem(x + d, 4)
        a4.append(send(rsb.at[yy, :, A], r2a.at[d - 1], YP[d - 1]))
        b4.append(send(rsb.at[:, xx, B], r2b.at[d - 1], XP[d - 1]))
    for cp in a4:
        cp.wait_recv()
    t4 = rsb[y, :, 0:56, :]
    for d in range(3):
        t4 += r2a[d]
    s3a[...] = t4
    a5 = [send(s3a.at[lax.rem(x + d, 4)], r3.at[d - 1, A], XP[d - 1]) for d in (2, 1, 3)]
    for cp in b4:
        cp.wait_recv()
    t4 = rsb[:, x, 56:104, :]
    for d in range(3):
        t4 += r2b[d]
    s3b[...] = t4
    b5 = [send(s3b.at[lax.rem(y + d, 4)], r3.at[d - 1, B], YP[d - 1]) for d in (2, 1, 3)]
    for cp in a5:
        cp.wait_recv()
    ta = s3a[x]
    for d in range(3):
        ta += r3[d, 0:56]
    for cp in b5:
        cp.wait_recv()
    tb = s3b[y]
    for d in range(3):
        tb += r3[d, 56:104]
    done = jnp.concatenate([ta, tb, jnp.zeros((8, 128), F32)], axis=0).astype(BF)
    out[c, z, y, x] = done
    S = (pl.ds(0, 48), pl.ds(48, 32), pl.ds(80, 32))
    w0, w1, w2 = (out.at[c, z, y, x, s] for s in S)
    st1 = [[send(w, w, p) for p in P] for w, P in ((w0, XP), (w1, YP), (w2, ZP))]
    w0, w1, w2 = out.at[c, z, y, :, S[0]], out.at[c, z, :, x, S[1]], out.at[c, :, y, x, S[2]]
    st2 = []
    for i, (w, P) in enumerate(((w0, YP), (w1, ZP), (w2, XP))):
        for cp in st1[i]:
            cp.wait_recv()
        st2.append([send(w, w, p) for p in P])
    w0, w1, w2 = out.at[c, z, :, :, S[0]], out.at[c, :, :, x, S[1]], out.at[c, :, y, :, S[2]]
    st3, last = [], []
    for i, (w, P) in enumerate(((w0, ZP), (w1, XP), (w2, YP))):
        for cp in st2[i]:
            cp.wait_recv()
        st3.append([send(w, w, P[d]) for d in (1, 0, 2)])
        last.append(send(w, w, CP))
    for i in range(3):
        for j, d in ((1, 1), (2, 3), (0, 2)):
            st3[i][j].wait_recv()
            if i == 0:
                w = out.at[c, lax.rem(z - d + 4, 4), :, :, S[0]]
            elif i == 1:
                w = out.at[c, :, :, lax.rem(x - d + 4, 4), S[1]]
            else:
                w = out.at[c, :, lax.rem(y - d + 4, 4), :, S[2]]
            last.append(send(w, w, CP))
    for cp in last:
        cp.wait_recv()
    for cp in sent:
        cp.wait_send()


def reduce_all(rows, rel, bpart):
    sem = pltpu.SemaphoreType.DMA
    v = pltpu.VMEM
    return pl.pallas_call(
        reduce_kernel,
        out_shape=jax.ShapeDtypeStruct((2, 4, 4, 4, 112, 128), BF),
        in_specs=[VM] * 3,
        out_specs=VM,
        scratch_shapes=[
            v((8, 224, TRIP), BF), v((8, 1, TRIP), jnp.int32), v((8, 56, 128), F32), v((8, 104, 256), F32),
            v((4, 4, 104, 128), F32), v((3, 4, 56, 128), F32), v((3, 4, 48, 128), F32),
            v((4, 56, 128), F32), v((4, 48, 128), F32), v((3, 104, 128), F32),
            sem((80,)), sem((80,)), sem((3,)),
        ],
        compiler_params=pltpu.CompilerParams(collective_id=1, has_side_effects=True, vmem_limit_bytes=40 * 2**20),
        cost_estimate=pl.CostEstimate(flops=8 * 10**10, bytes_accessed=10**7, transcendentals=0),
        name="reduce",
    )(rows, rel, bpart)


def unpack_kernel(tiles, coef_out, bases_out):
    r = pl.program_id(0)
    z, c = r // 2, r % 2
    for q in range(15):
        coef_out[:, q * 128 : (q + 1) * 128] = tiles[c, z, q // 4, q % 4, 0:NB].astype(F32)

    @pl.when(r == 0)
    def _():
        for j in range(8):
            n = min(56, D - 56 * j)
            if n > 0:
                bases_out[56 * j : 56 * j + n, :] = tiles[j % 2, j // 2, 3, 3, 0:n, 0:NB].astype(F32)


def unpack(tiles):
    return pl.pallas_call(
        unpack_kernel,
        grid=(8,),
        out_shape=(jax.ShapeDtypeStruct((NB, NREL), F32), jax.ShapeDtypeStruct((D, NB), F32)),
        in_specs=[pl.BlockSpec((2, 4, 4, 4, 112, 128), lambda i: (0,) * 6)],
        out_specs=(pl.BlockSpec((NB, RANGE), lambda i: (0, i)), pl.BlockSpec((D, NB), lambda i: (0, 0))),
        compiler_params=pltpu.CompilerParams(vmem_limit_bytes=40 * 2**20),
        name="unpack",
    )(tiles)


def per_device(head_emb, tail_emb, relation, owners, owner_rows, entities, neg_rows, coef, bases):
    rel = relation.reshape(1, TRIP)
    own_neg, grads, rows, bases_part, pos = score(
        head_emb.T, tail_emb.T, rel, owners.T, neg_rows, bases.T, coef.T, entities.T
    )
    packed = pack(pos, owner_rows.T, grads)
    recv = lax.all_to_all(packed, ("grp", "dev"), split_axis=0, concat_axis=0, tiled=True)
    tiles = reduce_all(rows, rel, bases_part)
    coef_grad, bases_grad = unpack(tiles)
    ent_grad = place(recv, own_neg, neg_rows)
    return ent_grad.T, coef_grad.T, bases_grad.T


def solution(mesh):
    rows = P(("grp", "dev"), None)
    return jax.shard_map(
        per_device,
        mesh=mesh,
        in_specs=(rows, rows, P(("grp", "dev")), rows, rows, rows, P(None, ("grp", "dev")), P(), P()),
        out_specs=(rows, P(), P()),
        check_vma=False,
    )
```

```python
import functools

import jax
import jax.numpy as jnp
from jax import lax
from jax.experimental import pallas as pl
from jax.experimental.pallas import tpu as pltpu
from jax.sharding import PartitionSpec as P

MESH = pl.DeviceIdType.MESH
HIGHEST = lax.Precision.HIGHEST
D = 400
NB = 100
TRIP = 1024
NEG = 128
ENT = 4096
NREL = 14824
GROUP = 32
NEG_ALL = NEG * GROUP
RA = (0, 208)
RB = (208, 192)
LOROW = 112
VM = pl.BlockSpec(memory_space=pltpu.VMEM)
ANY = pl.BlockSpec(memory_space=pl.ANY)
BF = jnp.bfloat16
F32 = jnp.float32


def dot(a, b, ca=1, cb=0, precision=None):
    return lax.dot_general(
        a, b, (((ca,), (cb,)), ((), ())), preferred_element_type=F32, precision=precision
    )


def spread(ids, rows):
    return (lax.broadcasted_iota(jnp.int32, (rows, ids.shape[1]), 0) == ids).astype(F32).astype(BF)


def equals(ids, value):
    return (ids == value).astype(F32).astype(BF)


def score_kernel(
    head, tail, rel, owners, negr, basest, coeft, entt,
    own_neg, grads, rows, bases_part, pos,
    coefv, entv, st, oh, pk, picked, relv, hrt, hr, mix, got, grd, pair, r2a, r2b, s3a, s3b, r3, blk,
    ss, rs, loc,
):
    g, k = lax.axis_index("grp"), lax.axis_index("dev")
    x, y, c = k // 8, lax.rem(k // 2, 4), lax.rem(k, 2)

    def dev(dx, dy, dc):
        return (g, (lax.rem(x + dx, 4) * 4 + lax.rem(y + dy, 4)) * 2 + lax.rem(c + dc, 2))

    get_ent = pltpu.make_async_copy(entt, entv, loc.at[0])
    get_ent.start()
    get_coef = pltpu.make_async_copy(coeft, coefv, loc.at[1])
    get_coef.start()
    bar = pltpu.get_barrier_semaphore()
    XP = [dev(d, 0, 0) for d in (1, 2, 3)]
    YP = [dev(0, d, 0) for d in (1, 2, 3)]
    CP = dev(0, 0, 1)
    for p in XP + YP + [CP]:
        pl.semaphore_signal(bar, inc=1, device_id=p, device_id_type=MESH)
    count = [0]
    sent = []

    def send(src, dst, p):
        i = count[0]
        count[0] += 1
        cp = pltpu.make_async_remote_copy(
            src_ref=src, dst_ref=dst, send_sem=ss.at[i], recv_sem=rs.at[i], device_id=p, device_id_type=MESH
        )
        cp.start()
        sent.append(cp)
        return cp

    pick_neg = spread(negr[...], ENT)
    get_ent.wait()
    got[c, y, x] = dot(entv[...], pick_neg).astype(BF)
    pl.semaphore_wait(bar, 7)
    A, B = pl.ds(*RA), pl.ds(*RB)
    mine_a, mine_b = got.at[c, y, x, A], got.at[c, y, x, B]
    a1 = [send(mine_a, mine_a, XP[d]) for d in (1, 0, 2)]
    b1 = [send(mine_b, mine_b, YP[d]) for d in (1, 0, 2)]

    st[...] = jnp.zeros_like(st)
    pk[...] = jnp.zeros_like(pk)
    ids = rel[...]
    low = spread(ids & 255, 256)
    high = lax.shift_right_logical(ids, 8)
    get_coef.wait()

    def load_coef(base, width, at):
        part = coefv[:, pl.ds(base, width)]
        first = part.astype(BF)
        st[0:NB, at : at + width] = first
        st[LOROW : LOROW + NB, at : at + width] = (part - first.astype(F32)).astype(BF)

    def gather(step):
        base = pl.multiple_of(step * 1024, 1024)
        load_coef(base, 1024, 0)
        for q in range(4):
            oh[q * 256 : (q + 1) * 256, :] = low * equals(high, step * 4 + q)
        pk[...] += dot(st[...], oh[...])

    def gather_loop(start, stop):
        def body(i, carry):
            gather(i)
            return carry

        lax.fori_loop(start, stop, body, 0)

    gather_loop(0, 5)
    for cp in a1:
        cp.wait_recv()
    line_a = got.at[c, y, :, A]
    a2 = [send(line_a, line_a, YP[d]) for d in (1, 0, 2)]
    for cp in b1:
        cp.wait_recv()
    line_b = got.at[c, :, x, B]
    b2 = [send(line_b, line_b, XP[d]) for d in (1, 0, 2)]
    last = [send(line_a, line_a, CP), send(line_b, line_b, CP)]

    gather_loop(5, 14)
    full = NREL // 1024 * 1024
    rest = NREL - full - 256
    load_coef(full, 256, 0)
    load_coef(full + 256, rest, 256)
    for q in range(2):
        oh[q * 256 : (q + 1) * 256, :] = low * equals(high, full // 256 + q)
    pk[...] += dot(st[:, 0 : 256 + rest], oh[0 : 256 + rest, :])
    chosen = pk[0:NB] + pk[LOROW : LOROW + NB]
    picked[...] = chosen
    relv[...] = dot(basest[...], chosen, precision=HIGHEST)
    hb = (head[...].astype(F32) * relv[...]).astype(BF)
    hrt[...] = hb
    hr[...] = hb.T
    tri = (
        lax.broadcasted_iota(jnp.int32, (256, 256), 0) < lax.broadcasted_iota(jnp.int32, (256, 256), 1)
    ).astype(F32).astype(BF)
    before = jnp.zeros((128, 1), F32)
    for h in range(2):
        for b in range(4):
            o = owners[h : h + 1, b * 256 : (b + 1) * 256]
            one = spread(o, 128)
            onef = one.astype(F32)
            rank = jnp.sum((dot(one, tri) + before) * onef, axis=0, keepdims=True)
            before = before + jnp.sum(onef, axis=1, keepdims=True)
            chip = lax.shift_right_logical(o, 1)
            pos[h : h + 1, b * 256 : (b + 1) * 256] = (
                lax.shift_right_logical(chip, 1) * 128
                + lax.rem((chip & 1) + c, 2) * 64
                + lax.rem((o & 1) + y, 2) * 32
                + rank.astype(jnp.int32)
            )

    for j, d in ((1, 1), (2, 3), (0, 2)):
        a2[j].wait_recv()
        r = got.at[c, lax.rem(y - d + 4, 4), :, A]
        last.append(send(r, r, CP))
        b2[j].wait_recv()
        r = got.at[c, :, lax.rem(x - d + 4, 4), B]
        last.append(send(r, r, CP))
    for cp in last:
        cp.wait_recv()

    mix[...] = jnp.zeros_like(mix)

    def chunk(cc, yy):
        for q in range(4):
            blk[:, q * 128 : (q + 1) * 128] = got[cc, yy, q]
        n = blk[...]
        s = dot(hr[...], n)
        prob = (0.5 * jnp.tanh(0.5 * s) + 0.5).astype(BF)
        mix[...] += dot(n, prob, 1, 1)
        part = (dot(hrt[...], prob) * (1.0 / NEG_ALL)).astype(BF)
        for q in range(4):
            grd[cc, yy, q] = part[:, q * 128 : (q + 1) * 128]

    halves = []
    for s in range(4):
        yy = lax.rem(y + 1 + s, 4)
        chunk(1 - c, yy)
        halves.append(send(grd.at[1 - c, yy], pair.at[yy], CP))
    a4, b4 = [], []
    for s in range(4):
        yy = lax.rem(y + 1 + s, 4)
        chunk(c, yy)
        halves[s].wait_recv()
        grd[c, yy] = (grd[c, yy].astype(F32) + pair[yy].astype(F32)).astype(BF)
        if s < 3:
            a4.append(send(grd.at[c, yy, :, A], r2a.at[s], YP[s]))
        for d in (1, 2, 3):
            xx = lax.rem(x + d, 4)
            b4.append(send(grd.at[c, yy, xx, B], r2b.at[d - 1, yy], XP[d - 1]))

    h, t = head[...].astype(F32), tail[...].astype(F32)
    rv = relv[...]
    hrv = h * rv
    score = jnp.sum(hrv * t, axis=0, keepdims=True)
    gate = 0.5 - 0.5 * jnp.tanh(0.5 * score)
    mean = mix[...] * (1.0 / NEG_ALL)
    inner = mean - gate * t
    grads[0] = (rv * inner).astype(BF)
    grads[1] = (-gate * hrv).astype(BF)
    rg = h * inner

    for cp in a4:
        cp.wait_recv()
    tot = grd[c, y, :, 0:208, :].astype(F32)
    for d in range(3):
        tot += r2a[d].astype(F32)
    s3a[...] = tot.astype(BF)
    a5 = [send(s3a.at[lax.rem(x + d, 4)], r3.at[d - 1, A], XP[d - 1]) for d in (1, 2, 3)]
    for cp in b4:
        cp.wait_recv()
    tot = grd[c, :, x, 208:400, :].astype(F32)
    for d in range(3):
        tot += r2b[d].astype(F32)
    s3b[...] = tot.astype(BF)
    b5 = [send(s3b.at[lax.rem(y + d, 4)], r3.at[d - 1, B], YP[d - 1]) for d in (1, 2, 3)]

    crow = dot(basest[...], rg, 0, 0, precision=HIGHEST)
    first = crow.astype(BF)
    rows[...] = jnp.zeros_like(rows)
    rows[0:NB] = first
    rows[LOROW : LOROW + NB] = (crow - first.astype(F32)).astype(BF)
    bases_part[...] = jnp.zeros_like(bases_part)
    bases_part[0:D, 0:NB] = dot(rg, picked[...], 1, 1, precision=HIGHEST)

    for cp in a5:
        cp.wait_recv()
    tot = s3a[x].astype(F32)
    for d in range(3):
        tot += r3[d, 0:208].astype(F32)
    own_neg[0:208] = tot
    for cp in b5:
        cp.wait_recv()
    tot = s3b[y].astype(F32)
    for d in range(3):
        tot += r3[d, 208:400].astype(F32)
    own_neg[208:400] = tot
    for cp in sent:
        cp.wait_send()


def score(head, tail, rel, owners, negr, basest, coeft, entt):
    sem = pltpu.SemaphoreType.DMA
    v = pltpu.VMEM
    return pl.pallas_call(
        score_kernel,
        out_shape=(
            jax.ShapeDtypeStruct((D, NEG), F32),
            jax.ShapeDtypeStruct((2, D, TRIP), BF),
            jax.ShapeDtypeStruct((224, TRIP), BF),
            jax.ShapeDtypeStruct((448, 128), F32),
            jax.ShapeDtypeStruct((2, TRIP), jnp.int32),
        ),
        in_specs=[VM] * 6 + [ANY] * 2,
        out_specs=(VM,) * 5,
        scratch_shapes=[
            v((NB, NREL), F32), v((D, ENT), BF), v((224, 1024), BF), v((1024, TRIP), BF), v((224, TRIP), F32),
            v((NB, TRIP), F32), v((D, TRIP), F32), v((D, TRIP), BF), v((TRIP, D), BF), v((D, TRIP), F32),
            v((2, 4, 4, D, NEG), BF), v((2, 4, 4, D, NEG), BF), v((4, 4, D, NEG), BF),
            v((3, 4, 208, NEG), BF), v((3, 4, 192, NEG), BF), v((4, 208, NEG), BF), v((4, 192, NEG), BF),
            v((3, D, NEG), BF), v((D, 512), BF),
            sem((48,)), sem((48,)), sem((2,)),
        ],
        compiler_params=pltpu.CompilerParams(collective_id=0, has_side_effects=True, vmem_limit_bytes=56 * 2**20),
        cost_estimate=pl.CostEstimate(flops=10**11, bytes_accessed=10**7, transcendentals=4 * 10**6),
        name="score",
    )(head, tail, rel, owners, negr, basest, coeft, entt)


WIDE = 4096 + 2 * NEG
HALF = 208


def place_kernel(recv, own_neg, negr, out, rt, low, ids):
    step = pl.program_id(0)

    @pl.when(step == 0)
    def _():
        rt[0:HALF, 0:4096] = recv[0]
        rt[HALF:D, 0:4096] = recv[1, 0 : D - HALF]
        a = recv[1, D - HALF : HALF].astype(F32)
        ids[:, 0:4096] = (a[0:1] * 64.0 + a[1:2]).astype(jnp.int32)
        n = own_neg[...]
        first = n.astype(BF)
        rt[0:D, 4096 : 4096 + NEG] = first
        rt[0:D, 4096 + NEG : WIDE] = (n - first.astype(F32)).astype(BF)
        ids[:, 4096 : 4096 + NEG] = negr[...]
        ids[:, 4096 + NEG : WIDE] = negr[...]
        low[...] = spread(ids[...] & 255, 256)

    one = low[...] * equals(lax.shift_right_logical(ids[...], 8), step)
    out[...] = dot(rt[0:D, :], one, 1, 1)


def place(recv, own_neg, negr):
    whole = lambda *s: pl.BlockSpec(s, lambda i: (0,) * len(s))
    return pl.pallas_call(
        place_kernel,
        grid=(16,),
        out_shape=jax.ShapeDtypeStruct((D, ENT), F32),
        in_specs=[whole(2, HALF, 4096), whole(D, NEG), whole(1, NEG)],
        out_specs=pl.BlockSpec((D, 256), lambda i: (0, i)),
        scratch_shapes=[pltpu.VMEM((D, WIDE), BF), pltpu.VMEM((256, WIDE), BF), pltpu.VMEM((1, WIDE), jnp.int32)],
        compiler_params=pltpu.CompilerParams(vmem_limit_bytes=40 * 2**20),
        cost_estimate=pl.CostEstimate(flops=14 * 10**9, bytes_accessed=11 * 10**6, transcendentals=0),
        name="place",
    )(recv, own_neg, negr)


RANGE = 1920


def exchange_kernel(
    rows, rel, bpart, pos, orow, grads, out, recv,
    gr, gi, gb, acc, rsb, r2a, r2b, s3a, s3b, r3,
    gx, low, pk, pb, w, v, u, xx, px, ss, rs, loc,
):
    z, k = lax.axis_index("grp"), lax.axis_index("dev")
    x, y, c = k // 8, lax.rem(k // 2, 4), lax.rem(k, 2)
    own = z * 2 + c

    def dev(dx, dy, dz, dc):
        return (lax.rem(z + dz, 4), (lax.rem(x + dx, 4) * 4 + lax.rem(y + dy, 4)) * 2 + lax.rem(c + dc, 2))

    XP = [dev(d, 0, 0, 0) for d in (1, 2, 3)]
    YP = [dev(0, d, 0, 0) for d in (1, 2, 3)]
    ZP = [dev(0, 0, d, 0) for d in (1, 2, 3)]
    ZC = [dev(0, 0, d, 1) for d in (1, 2, 3)]
    CP = dev(0, 0, 0, 1)
    xs = [lax.rem(x + d, 4) for d in range(4)]
    ys = [lax.rem(y + d, 4) for d in range(4)]
    zs = [lax.rem(z + d, 4) for d in range(4)]
    bar = pltpu.get_barrier_semaphore()
    for p in XP + YP + ZP + ZC + [CP]:
        pl.semaphore_signal(bar, inc=1, device_id=p, device_id_type=MESH)
    local = []

    def keep(src, dst):
        cp = pltpu.make_async_copy(src, dst, loc.at[len(local)])
        cp.start()
        local.append(cp)
        return cp

    kept = [
        keep(rows, gr.at[own]),
        keep(rel, gi.at[own]),
        keep(bpart.at[pl.ds(pl.multiple_of(own * 56, 8), 56)], gb.at[own]),
    ]
    count = [16]
    sent = []

    def remote(src, dst, i, p):
        return pltpu.make_async_remote_copy(
            src_ref=src, dst_ref=dst, send_sem=ss.at[i], recv_sem=rs.at[i], device_id=p, device_id_type=MESH
        )

    def send(src, dst, p):
        cp = remote(src, dst, count[0], p)
        count[0] += 1
        cp.start()
        sent.append(cp)
        return cp

    for h in range(2):
        at = h * TRIP
        low[:, at : at + TRIP] = spread(pos[h : h + 1] & 255, 256)
        r = orow[h : h + 1]
        two = lax.broadcasted_iota(jnp.int32, (16, TRIP), 0)
        extra = jnp.where(two == 0, lax.shift_right_logical(r, 6), jnp.where(two == 1, r & 63, 0))
        gx[0:D, at : at + TRIP] = grads[h]
        gx[D : D + 16, at : at + TRIP] = extra.astype(F32).astype(BF)
    for cp in kept:
        cp.wait()
    pl.semaphore_wait(bar, 13)
    first = [[send(rel, gi.at[own], ZP[d]), send(rows, gr.at[own], ZP[d])] for d in (0, 2, 1)]
    near = [send(rel, gi.at[own], CP), send(rows, gr.at[own], CP)]
    pieces = []

    def piece(dz, dc, p):
        r = zs[dz] * 2 + lax.rem(c + dc, 2)
        pieces.append(send(bpart.at[pl.ds(pl.multiple_of(r * 56, 8), 56)], gb.at[own], p))

    piece(0, 1, CP)
    for d in (1, 2, 3):
        piece(d, 0, ZP[d - 1])
        piece(d, 1, ZC[d - 1])

    S = (pl.ds(0, 80), pl.ds(80, 64), pl.ds(144, 64))
    high = [lax.shift_right_logical(pos[h : h + 1], 8) for h in range(2)]
    lane = lax.broadcasted_iota(jnp.int32, (HALF, 128), 1)
    side = (lane // 64) == c
    st1 = [[], [], []]

    def swap(s):
        return remote(pk.at[1 - c, s], pb.at[s], s, CP)

    for gp in range(4):
        zz = zs[(gp + 1) % 4]

        def fill(j, carry):
            s = zz * 4 + j
            tot = None
            for h in range(2):
                at = h * TRIP
                one = low[:, at : at + TRIP] * equals(high[h], s)
                d = dot(gx[:, at : at + TRIP], one, 1, 1)
                tot = d if tot is None else tot + d
            pk[0, s] = tot[0:HALF].astype(BF)
            pk[1, s] = tot[HALF : 2 * HALF].astype(BF)
            swap(s).start()
            return carry

        def join(j, carry):
            s = zz * 4 + j
            swap(s).wait()
            for q in range(2):
                a = pk[c, s, :, q * 128 : (q + 1) * 128]
                b = pb[s, :, q * 128 : (q + 1) * 128]
                w[zz, j, 2 * q] = jnp.where(side, a, b)
                w[zz, j, 2 * q + 1] = jnp.where(side, b, a)
            return carry

        lax.fori_loop(0, 4, fill, 0)
        lax.fori_loop(0, 4, join, 0)
        for d in (1, 3, 2):
            st1[0].append(send(w.at[zz, xs[d], :, S[0]], v.at[zz, x, :, S[0]], XP[d - 1]))
            st1[1].append(send(w.at[zz, :, ys[d], S[1]], v.at[zz, :, y, S[1]], YP[d - 1]))
        if gp < 3:
            st1[2].append(send(w.at[zz, :, :, S[2]], v.at[z, :, :, S[2]], ZP[gp]))
    st1[0].append(keep(w.at[:, x, :, S[0]], v.at[:, x, :, S[0]]))
    st1[1].append(keep(w.at[:, :, y, S[1]], v.at[:, :, y, S[1]]))
    st1[2].append(keep(w.at[z, :, :, S[2]], v.at[z, :, :, S[2]]))

    def arrived(cps):
        for cp in cps[:-1]:
            cp.wait_recv()
        cps[-1].wait()

    def along_x(a, b, s):
        cps = [send(a.at[:, xs[d], :, s], b.at[:, x, :, s], XP[d - 1]) for d in (1, 3, 2)]
        return cps + [keep(a.at[:, x, :, s], b.at[:, x, :, s])]

    def along_y(a, b, s):
        cps = [send(a.at[:, :, ys[d], s], b.at[:, :, y, s], YP[d - 1]) for d in (1, 3, 2)]
        return cps + [keep(a.at[:, :, y, s], b.at[:, :, y, s])]

    def along_z(a, b, s):
        cps = [send(a.at[zs[d], :, :, s], b.at[z, :, :, s], ZP[d - 1]) for d in (1, 3, 2)]
        return cps + [keep(a.at[z, :, :, s], b.at[z, :, :, s])]

    def add(j, start):
        ids = gi[j] - own * RANGE
        lo = spread(ids & 255, 256)
        hi = lax.shift_right_arithmetic(ids, 8)
        r = gr[j]
        for t in range(8):
            p = dot(r * equals(hi, t), lo, 1, 1)
            p = p[0:104] + p[LOROW : LOROW + 104]
            if start:
                acc[t] = p
            else:
                acc[t] += p

    add(own, True)
    for cp in near:
        cp.wait_recv()
    add(z * 2 + 1 - c, False)

    st2 = []
    for i, go in enumerate((along_y, along_z, along_x)):
        arrived(st1[i])
        st2.append(go(v, u, S[i]))

    for i, d in enumerate((1, 3, 2)):
        from_z = lax.rem(z - d + 4, 4) * 2
        for cp in first[i]:
            cp.wait_recv()
        more = [send(gi.at[from_z + c], gi.at[from_z + c], CP), send(gr.at[from_z + c], gr.at[from_z + c], CP)]
        add(from_z + c, False)
        for cp in more:
            cp.wait_recv()
        add(from_z + 1 - c, False)
    for cp in pieces:
        cp.wait_recv()
    tot = gb[0]
    for j in range(1, 8):
        tot += gb[j]
    for q in range(16):
        if q == 15:
            rsb[3, 3] = jnp.zeros((104, 128), F32)
            rsb[3, 3, 0:56] = tot
        else:
            rsb[q // 4, q % 4] = acc[q // 2, :, (q % 2) * 128 : (q % 2) * 128 + 128]

    st3 = []
    for i, go in enumerate((along_z, along_x, along_y)):
        arrived(st2[i])
        st3.append(go(u, xx, S[i]))

    A, B = pl.ds(0, 56), pl.ds(56, 48)
    a4, b4 = [], []
    for d in (2, 1, 3):
        a4.append(send(rsb.at[ys[d], :, A], r2a.at[d - 1], YP[d - 1]))
        b4.append(send(rsb.at[:, xs[d], B], r2b.at[d - 1], XP[d - 1]))
    for cp in a4:
        cp.wait_recv()
    t4 = rsb[y, :, 0:56, :]
    for d in range(3):
        t4 += r2a[d]
    s3a[...] = t4
    a5 = [send(s3a.at[xs[d]], r3.at[d - 1, A], XP[d - 1]) for d in (2, 1, 3)]
    for cp in b4:
        cp.wait_recv()
    t4 = rsb[:, x, 56:104, :]
    for d in range(3):
        t4 += r2b[d]
    s3b[...] = t4
    b5 = [send(s3b.at[ys[d]], r3.at[d - 1, B], YP[d - 1]) for d in (2, 1, 3)]
    for cp in a5:
        cp.wait_recv()
    ta = s3a[x]
    for d in range(3):
        ta += r3[d, 0:56]
    for cp in b5:
        cp.wait_recv()
    tb = s3b[y]
    for d in range(3):
        tb += r3[d, 56:104]
    done = jnp.concatenate([ta, tb, jnp.zeros((8, 128), F32)], axis=0).astype(BF)
    out[c, z, y, x] = done
    T = (pl.ds(0, 48), pl.ds(48, 32), pl.ds(80, 32))
    w0, w1, w2 = (out.at[c, z, y, x, s] for s in T)
    g1 = [[send(q, q, p) for p in Q] for q, Q in ((w0, XP), (w1, YP), (w2, ZP))]
    w0, w1, w2 = out.at[c, z, y, :, T[0]], out.at[c, z, :, x, T[1]], out.at[c, :, y, x, T[2]]
    g2 = []
    for i, (q, Q) in enumerate(((w0, YP), (w1, ZP), (w2, XP))):
        for cp in g1[i]:
            cp.wait_recv()
        g2.append([send(q, q, p) for p in Q])
    w0, w1, w2 = out.at[c, z, :, :, T[0]], out.at[c, :, :, x, T[1]], out.at[c, :, y, :, T[2]]
    g3, last = [], []
    for i, (q, Q) in enumerate(((w0, ZP), (w1, XP), (w2, YP))):
        for cp in g2[i]:
            cp.wait_recv()
        g3.append([send(q, q, Q[d]) for d in (1, 0, 2)])
        last.append(send(q, q, CP))

    for i in range(3):
        arrived(st3[i])
    unit = (lax.rem(lane // 32, 2) == 0) == (c == 0)
    final = []
    for zz in range(4):

        def part(xi, carry):
            for q in range(2):
                a, b = xx[zz, xi, 2 * q], xx[zz, xi, 2 * q + 1]
                at = pl.ds(pl.multiple_of(zz * 1024 + xi * 256 + q * 128, 128), 128)
                recv[c, :, at] = jnp.where(unit, a, b)
                px[:, at] = jnp.where(unit, b, a)
            return carry

        lax.fori_loop(0, 4, part, 0)
        span = pl.ds(zz * 1024, 1024)
        final.append(send(px.at[:, span], recv.at[c, :, span], CP))

    for i in range(3):
        for j, d in ((1, 1), (2, 3), (0, 2)):
            g3[i][j].wait_recv()
            if i == 0:
                q = out.at[c, lax.rem(z - d + 4, 4), :, :, T[0]]
            elif i == 1:
                q = out.at[c, :, :, lax.rem(x - d + 4, 4), T[1]]
            else:
                q = out.at[c, :, lax.rem(y - d + 4, 4), :, T[2]]
            last.append(send(q, q, CP))
    for cp in last + final:
        cp.wait_recv()
    for cp in sent:
        cp.wait_send()


def exchange(rows, rel, bpart, pos, orow, grads):
    sem = pltpu.SemaphoreType.DMA
    v = pltpu.VMEM
    big = (4, 4, 4, HALF, 128)
    return pl.pallas_call(
        exchange_kernel,
        out_shape=(
            jax.ShapeDtypeStruct((2, 4, 4, 4, 112, 128), BF),
            jax.ShapeDtypeStruct((2, HALF, 4096), BF),
        ),
        in_specs=[VM] * 6,
        out_specs=(VM, VM),
        scratch_shapes=[
            v((8, 224, TRIP), BF), v((8, 1, TRIP), jnp.int32), v((8, 56, 128), F32), v((8, 104, 256), F32),
            v((4, 4, 104, 128), F32), v((3, 4, 56, 128), F32), v((3, 4, 48, 128), F32),
            v((4, 56, 128), F32), v((4, 48, 128), F32), v((3, 104, 128), F32),
            v((2 * HALF, 2 * TRIP), BF), v((256, 2 * TRIP), BF), v((2, 16, HALF, 256), BF), v((16, HALF, 256), BF),
            v(big, BF), v(big, BF), v(big, BF), v(big, BF), v((HALF, 4096), BF),
            sem((160,)), sem((160,)), sem((16,)),
        ],
        compiler_params=pltpu.CompilerParams(collective_id=1, has_side_effects=True, vmem_limit_bytes=56 * 2**20),
        cost_estimate=pl.CostEstimate(flops=8 * 10**10, bytes_accessed=10**7, transcendentals=0),
        name="exchange",
    )(rows, rel, bpart, pos, orow, grads)


def unpack_kernel(tiles, coef_out, bases_out):
    r = pl.program_id(0)
    z, c = r // 2, r % 2
    for q in range(15):
        coef_out[:, q * 128 : (q + 1) * 128] = tiles[c, z, q // 4, q % 4, 0:NB].astype(F32)

    @pl.when(r == 0)
    def _():
        for j in range(8):
            n = min(56, D - 56 * j)
            if n > 0:
                bases_out[56 * j : 56 * j + n, :] = tiles[j % 2, j // 2, 3, 3, 0:n, 0:NB].astype(F32)


def unpack(tiles):
    return pl.pallas_call(
        unpack_kernel,
        grid=(8,),
        out_shape=(jax.ShapeDtypeStruct((NB, NREL), F32), jax.ShapeDtypeStruct((D, NB), F32)),
        in_specs=[pl.BlockSpec((2, 4, 4, 4, 112, 128), lambda i: (0,) * 6)],
        out_specs=(pl.BlockSpec((NB, RANGE), lambda i: (0, i)), pl.BlockSpec((D, NB), lambda i: (0, 0))),
        compiler_params=pltpu.CompilerParams(vmem_limit_bytes=40 * 2**20),
        name="unpack",
    )(tiles)


def per_device(head_emb, tail_emb, relation, owners, owner_rows, entities, neg_rows, coef, bases):
    rel = relation.reshape(1, TRIP)
    own_neg, grads, rows, bases_part, pos = score(
        head_emb.T, tail_emb.T, rel, owners.T, neg_rows, bases.T, coef.T, entities.T
    )
    tiles, recv = exchange(rows, rel, bases_part, pos, owner_rows.T, grads)
    coef_grad, bases_grad = unpack(tiles)
    ent_grad = place(recv, own_neg, neg_rows)
    return ent_grad.T, coef_grad.T, bases_grad.T


def solution(mesh):
    rows = P(("grp", "dev"), None)
    return jax.shard_map(
        per_device,
        mesh=mesh,
        in_specs=(rows, rows, P(("grp", "dev")), rows, rows, rows, P(None, ("grp", "dev")), P(), P()),
        out_specs=(rows, P(), P()),
        check_vma=False,
    )
```

```python
import functools

import jax
import jax.numpy as jnp
from jax import lax
from jax.experimental import pallas as pl
from jax.experimental.pallas import tpu as pltpu
from jax.sharding import PartitionSpec as P

MESH = pl.DeviceIdType.MESH
HIGHEST = lax.Precision.HIGHEST
D = 400
NB = 100
TRIP = 1024
NEG = 128
ENT = 4096
NREL = 14824
GROUP = 32
NEG_ALL = NEG * GROUP
RA = (0, 208)
RB = (208, 192)
LOROW = 112
VM = pl.BlockSpec(memory_space=pltpu.VMEM)
ANY = pl.BlockSpec(memory_space=pl.ANY)
BF = jnp.bfloat16
F32 = jnp.float32


def dot(a, b, ca=1, cb=0, precision=None):
    return lax.dot_general(
        a, b, (((ca,), (cb,)), ((), ())), preferred_element_type=F32, precision=precision
    )


def spread(ids, rows):
    return (lax.broadcasted_iota(jnp.int32, (rows, ids.shape[1]), 0) == ids).astype(F32).astype(BF)


def equals(ids, value):
    return (ids == value).astype(F32).astype(BF)


def score_kernel(
    head, tail, rel, owners, negr, basest, coeft, entt,
    own_neg, grads, rows, bases_part, pos,
    coefv, entv, st, oh, pk, picked, relv, hrt, hr, mix, got, grd, pair, r2a, r2b, s3a, s3b, r3, blk,
    ss, rs, loc,
):
    g, k = lax.axis_index("grp"), lax.axis_index("dev")
    x, y, c = k // 8, lax.rem(k // 2, 4), lax.rem(k, 2)

    def dev(dx, dy, dc):
        return (g, (lax.rem(x + dx, 4) * 4 + lax.rem(y + dy, 4)) * 2 + lax.rem(c + dc, 2))

    get_ent = pltpu.make_async_copy(entt, entv, loc.at[0])
    get_ent.start()
    get_coef = pltpu.make_async_copy(coeft, coefv, loc.at[1])
    get_coef.start()
    bar = pltpu.get_barrier_semaphore()
    XP = [dev(d, 0, 0) for d in (1, 2, 3)]
    YP = [dev(0, d, 0) for d in (1, 2, 3)]
    CP = dev(0, 0, 1)
    for p in XP + YP + [CP]:
        pl.semaphore_signal(bar, inc=1, device_id=p, device_id_type=MESH)
    count = [0]
    sent = []

    def send(src, dst, p):
        i = count[0]
        count[0] += 1
        cp = pltpu.make_async_remote_copy(
            src_ref=src, dst_ref=dst, send_sem=ss.at[i], recv_sem=rs.at[i], device_id=p, device_id_type=MESH
        )
        cp.start()
        sent.append(cp)
        return cp

    pick_neg = spread(negr[...], ENT)
    get_ent.wait()
    got[c, y, x] = dot(entv[...], pick_neg).astype(BF)
    pl.semaphore_wait(bar, 7)
    A, B = pl.ds(*RA), pl.ds(*RB)
    mine_a, mine_b = got.at[c, y, x, A], got.at[c, y, x, B]
    a1 = [send(mine_a, mine_a, XP[d]) for d in (1, 0, 2)]
    b1 = [send(mine_b, mine_b, YP[d]) for d in (1, 0, 2)]

    st[...] = jnp.zeros_like(st)
    pk[...] = jnp.zeros_like(pk)
    ids = rel[...]
    low = spread(ids & 255, 256)
    high = lax.shift_right_logical(ids, 8)
    get_coef.wait()

    def load_coef(base, width, at):
        part = coefv[:, pl.ds(base, width)]
        first = part.astype(BF)
        st[0:NB, at : at + width] = first
        st[LOROW : LOROW + NB, at : at + width] = (part - first.astype(F32)).astype(BF)

    def gather(step):
        base = pl.multiple_of(step * 1024, 1024)
        load_coef(base, 1024, 0)
        for q in range(4):
            oh[q * 256 : (q + 1) * 256, :] = low * equals(high, step * 4 + q)
        pk[...] += dot(st[...], oh[...])

    def gather_loop(start, stop):
        def body(i, carry):
            gather(i)
            return carry

        lax.fori_loop(start, stop, body, 0)

    gather_loop(0, 5)
    for cp in a1:
        cp.wait_recv()
    line_a = got.at[c, y, :, A]
    a2 = [send(line_a, line_a, YP[d]) for d in (1, 0, 2)]
    for cp in b1:
        cp.wait_recv()
    line_b = got.at[c, :, x, B]
    b2 = [send(line_b, line_b, XP[d]) for d in (1, 0, 2)]
    last = [send(line_a, line_a, CP), send(line_b, line_b, CP)]

    gather_loop(5, 14)
    full = NREL // 1024 * 1024
    rest = NREL - full - 256
    load_coef(full, 256, 0)
    load_coef(full + 256, rest, 256)
    for q in range(2):
        oh[q * 256 : (q + 1) * 256, :] = low * equals(high, full // 256 + q)
    pk[...] += dot(st[:, 0 : 256 + rest], oh[0 : 256 + rest, :])
    chosen = pk[0:NB] + pk[LOROW : LOROW + NB]
    picked[...] = chosen
    relv[...] = dot(basest[...], chosen, precision=HIGHEST)
    hb = (head[...].astype(F32) * relv[...]).astype(BF)
    hrt[...] = hb
    hr[...] = hb.T
    tri = (
        lax.broadcasted_iota(jnp.int32, (256, 256), 0) < lax.broadcasted_iota(jnp.int32, (256, 256), 1)
    ).astype(F32).astype(BF)
    before = jnp.zeros((128, 1), F32)
    for h in range(2):
        for b in range(4):
            o = owners[h : h + 1, b * 256 : (b + 1) * 256]
            one = spread(o, 128)
            onef = one.astype(F32)
            rank = jnp.sum((dot(one, tri) + before) * onef, axis=0, keepdims=True)
            before = before + jnp.sum(onef, axis=1, keepdims=True)
            chip = lax.shift_right_logical(o, 1)
            pos[h : h + 1, b * 256 : (b + 1) * 256] = (
                lax.shift_right_logical(chip, 1) * 128
                + lax.rem((chip & 1) + c, 2) * 64
                + lax.rem((o & 1) + y, 2) * 32
                + rank.astype(jnp.int32)
            )

    for j, d in ((1, 1), (2, 3), (0, 2)):
        a2[j].wait_recv()
        r = got.at[c, lax.rem(y - d + 4, 4), :, A]
        last.append(send(r, r, CP))
        b2[j].wait_recv()
        r = got.at[c, :, lax.rem(x - d + 4, 4), B]
        last.append(send(r, r, CP))
    for cp in last:
        cp.wait_recv()

    mix[...] = jnp.zeros_like(mix)

    def chunk(cc, yy):
        for q in range(4):
            blk[:, q * 128 : (q + 1) * 128] = got[cc, yy, q]
        n = blk[...]
        s = dot(hr[...], n)
        prob = (0.5 * jnp.tanh(0.5 * s) + 0.5).astype(BF)
        mix[...] += dot(n, prob, 1, 1)
        part = (dot(hrt[...], prob) * (1.0 / NEG_ALL)).astype(BF)
        for q in range(4):
            grd[cc, yy, q] = part[:, q * 128 : (q + 1) * 128]

    halves = []
    for s in range(4):
        yy = lax.rem(y + 1 + s, 4)
        chunk(1 - c, yy)
        halves.append(send(grd.at[1 - c, yy], pair.at[yy], CP))
    a4, b4 = [], []
    for s in range(4):
        yy = lax.rem(y + 1 + s, 4)
        chunk(c, yy)
        halves[s].wait_recv()
        grd[c, yy] = (grd[c, yy].astype(F32) + pair[yy].astype(F32)).astype(BF)
        if s < 3:
            a4.append(send(grd.at[c, yy, :, A], r2a.at[s], YP[s]))
        for d in (1, 2, 3):
            xx = lax.rem(x + d, 4)
            b4.append(send(grd.at[c, yy, xx, B], r2b.at[d - 1, yy], XP[d - 1]))

    h, t = head[...].astype(F32), tail[...].astype(F32)
    rv = relv[...]
    hrv = h * rv
    score = jnp.sum(hrv * t, axis=0, keepdims=True)
    gate = 0.5 - 0.5 * jnp.tanh(0.5 * score)
    mean = mix[...] * (1.0 / NEG_ALL)
    inner = mean - gate * t
    grads[0] = (rv * inner).astype(BF)
    grads[1] = (-gate * hrv).astype(BF)
    rg = h * inner

    for cp in a4:
        cp.wait_recv()
    tot = grd[c, y, :, 0:208, :].astype(F32)
    for d in range(3):
        tot += r2a[d].astype(F32)
    s3a[...] = tot.astype(BF)
    a5 = [send(s3a.at[lax.rem(x + d, 4)], r3.at[d - 1, A], XP[d - 1]) for d in (1, 2, 3)]
    for cp in b4:
        cp.wait_recv()
    tot = grd[c, :, x, 208:400, :].astype(F32)
    for d in range(3):
        tot += r2b[d].astype(F32)
    s3b[...] = tot.astype(BF)
    b5 = [send(s3b.at[lax.rem(y + d, 4)], r3.at[d - 1, B], YP[d - 1]) for d in (1, 2, 3)]

    crow = dot(basest[...], rg, 0, 0, precision=HIGHEST)
    first = crow.astype(BF)
    rows[...] = jnp.zeros_like(rows)
    rows[0:NB] = first
    rows[LOROW : LOROW + NB] = (crow - first.astype(F32)).astype(BF)
    bases_part[...] = jnp.zeros_like(bases_part)
    bases_part[0:D, 0:NB] = dot(rg, picked[...], 1, 1, precision=HIGHEST)

    for cp in a5:
        cp.wait_recv()
    tot = s3a[x].astype(F32)
    for d in range(3):
        tot += r3[d, 0:208].astype(F32)
    own_neg[0:208] = tot
    for cp in b5:
        cp.wait_recv()
    tot = s3b[y].astype(F32)
    for d in range(3):
        tot += r3[d, 208:400].astype(F32)
    own_neg[208:400] = tot
    for cp in sent:
        cp.wait_send()


def score(head, tail, rel, owners, negr, basest, coeft, entt):
    sem = pltpu.SemaphoreType.DMA
    v = pltpu.VMEM
    return pl.pallas_call(
        score_kernel,
        out_shape=(
            jax.ShapeDtypeStruct((D, NEG), F32),
            jax.ShapeDtypeStruct((2, D, TRIP), BF),
            jax.ShapeDtypeStruct((224, TRIP), BF),
            jax.ShapeDtypeStruct((448, 128), F32),
            jax.ShapeDtypeStruct((2, TRIP), jnp.int32),
        ),
        in_specs=[VM] * 6 + [ANY] * 2,
        out_specs=(VM,) * 5,
        scratch_shapes=[
            v((NB, NREL), F32), v((D, ENT), BF), v((224, 1024), BF), v((1024, TRIP), BF), v((224, TRIP), F32),
            v((NB, TRIP), F32), v((D, TRIP), F32), v((D, TRIP), BF), v((TRIP, D), BF), v((D, TRIP), F32),
            v((2, 4, 4, D, NEG), BF), v((2, 4, 4, D, NEG), BF), v((4, 4, D, NEG), BF),
            v((3, 4, 208, NEG), BF), v((3, 4, 192, NEG), BF), v((4, 208, NEG), BF), v((4, 192, NEG), BF),
            v((3, D, NEG), BF), v((D, 512), BF),
            sem((48,)), sem((48,)), sem((2,)),
        ],
        compiler_params=pltpu.CompilerParams(collective_id=0, has_side_effects=True, vmem_limit_bytes=56 * 2**20),
        cost_estimate=pl.CostEstimate(flops=10**11, bytes_accessed=10**7, transcendentals=4 * 10**6),
        name="score",
    )(head, tail, rel, owners, negr, basest, coeft, entt)


WIDE = 4096 + 2 * NEG
HALF = 208


def place_kernel(recv, own_neg, negr, out, rt, low, ids):
    step = pl.program_id(0)

    @pl.when(step == 0)
    def _():
        rt[0:HALF, 0:4096] = recv[0]
        rt[HALF:D, 0:4096] = recv[1, 0 : D - HALF]
        a = recv[1, D - HALF : HALF].astype(F32)
        ids[:, 0:4096] = (a[0:1] * 64.0 + a[1:2]).astype(jnp.int32)
        n = own_neg[...]
        first = n.astype(BF)
        rt[0:D, 4096 : 4096 + NEG] = first
        rt[0:D, 4096 + NEG : WIDE] = (n - first.astype(F32)).astype(BF)
        ids[:, 4096 : 4096 + NEG] = negr[...]
        ids[:, 4096 + NEG : WIDE] = negr[...]
        for q in range(WIDE // 256):
            at = q * 256
            low[at : at + 256, :] = spread(ids[:, at : at + 256] & 255, 256).T

    for q in range(2):
        keep = equals(lax.shift_right_logical(ids[...], 8), step * 2 + q)
        out[:, q * 256 : (q + 1) * 256] = dot(rt[...] * keep, low[...])


def place(recv, own_neg, negr):
    whole = lambda *s: pl.BlockSpec(s, lambda i: (0,) * len(s))
    return pl.pallas_call(
        place_kernel,
        grid=(8,),
        out_shape=jax.ShapeDtypeStruct((D, ENT), F32),
        in_specs=[whole(2, HALF, 4096), whole(D, NEG), whole(1, NEG)],
        out_specs=pl.BlockSpec((D, 512), lambda i: (0, i)),
        scratch_shapes=[pltpu.VMEM((D, WIDE), BF), pltpu.VMEM((WIDE, 256), BF), pltpu.VMEM((1, WIDE), jnp.int32)],
        compiler_params=pltpu.CompilerParams(vmem_limit_bytes=40 * 2**20),
        cost_estimate=pl.CostEstimate(flops=14 * 10**9, bytes_accessed=11 * 10**6, transcendentals=0),
        name="place",
    )(recv, own_neg, negr)


RANGE = 1920


def exchange_kernel(
    rows, rel, bpart, pos, orow, grads, out, recv,
    gr, gi, gb, acc, rsb, r2a, r2b, s3a, s3b, r3,
    gx, low, pk, pb, w, v, u, xx, px, ss, rs, loc,
):
    z, k = lax.axis_index("grp"), lax.axis_index("dev")
    x, y, c = k // 8, lax.rem(k // 2, 4), lax.rem(k, 2)
    own = z * 2 + c

    def dev(dx, dy, dz, dc):
        return (lax.rem(z + dz, 4), (lax.rem(x + dx, 4) * 4 + lax.rem(y + dy, 4)) * 2 + lax.rem(c + dc, 2))

    XP = [dev(d, 0, 0, 0) for d in (1, 2, 3)]
    YP = [dev(0, d, 0, 0) for d in (1, 2, 3)]
    ZP = [dev(0, 0, d, 0) for d in (1, 2, 3)]
    ZC = [dev(0, 0, d, 1) for d in (1, 2, 3)]
    CP = dev(0, 0, 0, 1)
    xs = [lax.rem(x + d, 4) for d in range(4)]
    ys = [lax.rem(y + d, 4) for d in range(4)]
    zs = [lax.rem(z + d, 4) for d in range(4)]
    bar = pltpu.get_barrier_semaphore()
    for p in XP + YP + ZP + ZC + [CP]:
        pl.semaphore_signal(bar, inc=1, device_id=p, device_id_type=MESH)
    local = []

    def keep(src, dst):
        cp = pltpu.make_async_copy(src, dst, loc.at[len(local)])
        cp.start()
        local.append(cp)
        return cp

    kept = [
        keep(rows, gr.at[own]),
        keep(rel, gi.at[own]),
        keep(bpart.at[pl.ds(pl.multiple_of(own * 56, 8), 56)], gb.at[own]),
    ]
    count = [16]
    sent = []

    def remote(src, dst, i, p):
        return pltpu.make_async_remote_copy(
            src_ref=src, dst_ref=dst, send_sem=ss.at[i], recv_sem=rs.at[i], device_id=p, device_id_type=MESH
        )

    def send(src, dst, p):
        cp = remote(src, dst, count[0], p)
        count[0] += 1
        cp.start()
        sent.append(cp)
        return cp

    for h in range(2):
        at = h * TRIP
        low[:, at : at + TRIP] = spread(pos[h : h + 1] & 255, 256)
        r = orow[h : h + 1]
        two = lax.broadcasted_iota(jnp.int32, (16, TRIP), 0)
        extra = jnp.where(two == 0, lax.shift_right_logical(r, 6), jnp.where(two == 1, r & 63, 0))
        gx[0:D, at : at + TRIP] = grads[h]
        gx[D : D + 16, at : at + TRIP] = extra.astype(F32).astype(BF)
    for cp in kept:
        cp.wait()
    pl.semaphore_wait(bar, 13)
    first = [[send(rel, gi.at[own], p), send(rows, gr.at[own], p)] for p in (ZP[0], ZP[2])]
    zm, zp = zs[3] * 2 + c, zs[1] * 2 + c
    HI, LO = pl.ds(0, LOROW), pl.ds(LOROW, LOROW)

    def pass_on():
        for cp in first[0]:
            cp.wait_recv()
        away = [send(gi.at[zm], gi.at[zm], ZP[0]), send(gr.at[zm, HI], gr.at[zm, HI], ZP[0])]
        for cp in first[1]:
            cp.wait_recv()
        return away + [send(gr.at[zp, LO], gr.at[zp, LO], ZP[2])]

    near = [send(rel, gi.at[own], CP), send(rows, gr.at[own], CP)]
    pieces = []

    def piece(dz, dc, p):
        r = zs[dz] * 2 + lax.rem(c + dc, 2)
        pieces.append(send(bpart.at[pl.ds(pl.multiple_of(r * 56, 8), 56)], gb.at[own], p))

    piece(0, 1, CP)
    for d in (1, 2, 3):
        piece(d, 0, ZP[d - 1])
        piece(d, 1, ZC[d - 1])

    S = (pl.ds(0, 80), pl.ds(80, 64), pl.ds(144, 64))
    high = [lax.shift_right_logical(pos[h : h + 1], 8) for h in range(2)]
    lane = lax.broadcasted_iota(jnp.int32, (HALF, 128), 1)
    side = (lane // 64) == c
    st1 = [[], [], []]

    def swap(s):
        return remote(pk.at[1 - c, s], pb.at[s], s, CP)

    for gp in range(4):
        zz = zs[(gp + 1) % 4]

        def fill(j, carry):
            s = zz * 4 + j
            tot = None
            for h in range(2):
                at = h * TRIP
                one = low[:, at : at + TRIP] * equals(high[h], s)
                d = dot(gx[:, at : at + TRIP], one, 1, 1)
                tot = d if tot is None else tot + d
            pk[0, s] = tot[0:HALF].astype(BF)
            pk[1, s] = tot[HALF : 2 * HALF].astype(BF)
            swap(s).start()
            return carry

        def join(j, carry):
            s = zz * 4 + j
            swap(s).wait()
            for q in range(2):
                a = pk[c, s, :, q * 128 : (q + 1) * 128]
                b = pb[s, :, q * 128 : (q + 1) * 128]
                w[zz, j, 2 * q] = jnp.where(side, a, b)
                w[zz, j, 2 * q + 1] = jnp.where(side, b, a)
            return carry

        lax.fori_loop(0, 4, fill, 0)
        lax.fori_loop(0, 4, join, 0)
        for d in (1, 3, 2):
            st1[0].append(send(w.at[zz, xs[d], :, S[0]], v.at[zz, x, :, S[0]], XP[d - 1]))
            st1[1].append(send(w.at[zz, :, ys[d], S[1]], v.at[zz, :, y, S[1]], YP[d - 1]))
        if gp == 2:
            away = pass_on()
        if gp < 3:
            st1[2].append(send(w.at[zz, :, :, S[2]], v.at[z, :, :, S[2]], ZP[gp]))
    st1[0].append(keep(w.at[:, x, :, S[0]], v.at[:, x, :, S[0]]))
    st1[1].append(keep(w.at[:, :, y, S[1]], v.at[:, :, y, S[1]]))
    st1[2].append(keep(w.at[z, :, :, S[2]], v.at[z, :, :, S[2]]))

    def arrived(cps):
        for cp in cps[:-1]:
            cp.wait_recv()
        cps[-1].wait()

    def along_x(a, b, s):
        cps = [send(a.at[:, xs[d], :, s], b.at[:, x, :, s], XP[d - 1]) for d in (1, 3, 2)]
        return cps + [keep(a.at[:, x, :, s], b.at[:, x, :, s])]

    def along_y(a, b, s):
        cps = [send(a.at[:, :, ys[d], s], b.at[:, :, y, s], YP[d - 1]) for d in (1, 3, 2)]
        return cps + [keep(a.at[:, :, y, s], b.at[:, :, y, s])]

    def along_z(a, b, s):
        cps = [send(a.at[zs[d], :, :, s], b.at[z, :, :, s], ZP[d - 1]) for d in (1, 3, 2)]
        return cps + [keep(a.at[z, :, :, s], b.at[z, :, :, s])]

    def add(j, start):
        ids = gi[j] - own * RANGE
        lo = spread(ids & 255, 256)
        hi = lax.shift_right_arithmetic(ids, 8)
        r = gr[j]
        for t in range(8):
            p = dot(r * equals(hi, t), lo, 1, 1)
            p = p[0:104] + p[LOROW : LOROW + 104]
            if start:
                acc[t] = p
            else:
                acc[t] += p

    add(own, True)
    for cp in near:
        cp.wait_recv()
    add(z * 2 + 1 - c, False)

    st2 = []
    for i, go in enumerate((along_y, along_z, along_x)):
        arrived(st1[i])
        st2.append(go(v, u, S[i]))

    for i, d in enumerate((1, 3, 2)):
        from_z = zs[4 - d] * 2
        if i == 2:
            for cp in away:
                cp.wait_recv()
        more = [send(gi.at[from_z + c], gi.at[from_z + c], CP), send(gr.at[from_z + c], gr.at[from_z + c], CP)]
        add(from_z + c, False)
        for cp in more:
            cp.wait_recv()
        add(from_z + 1 - c, False)
    for cp in pieces:
        cp.wait_recv()
    tot = gb[0]
    for j in range(1, 8):
        tot += gb[j]
    for q in range(16):
        if q == 15:
            rsb[3, 3] = jnp.zeros((104, 128), F32)
            rsb[3, 3, 0:56] = tot
        else:
            rsb[q // 4, q % 4] = acc[q // 2, :, (q % 2) * 128 : (q % 2) * 128 + 128]

    st3 = []
    for i, go in enumerate((along_z, along_x, along_y)):
        arrived(st2[i])
        st3.append(go(u, xx, S[i]))

    A, B = pl.ds(0, 56), pl.ds(56, 48)
    a4, b4 = [], []
    for d in (2, 1, 3):
        a4.append(send(rsb.at[ys[d], :, A], r2a.at[d - 1], YP[d - 1]))
        b4.append(send(rsb.at[:, xs[d], B], r2b.at[d - 1], XP[d - 1]))
    for cp in a4:
        cp.wait_recv()
    t4 = rsb[y, :, 0:56, :]
    for d in range(3):
        t4 += r2a[d]
    s3a[...] = t4
    a5 = [send(s3a.at[xs[d]], r3.at[d - 1, A], XP[d - 1]) for d in (2, 1, 3)]
    for cp in b4:
        cp.wait_recv()
    t4 = rsb[:, x, 56:104, :]
    for d in range(3):
        t4 += r2b[d]
    s3b[...] = t4
    b5 = [send(s3b.at[ys[d]], r3.at[d - 1, B], YP[d - 1]) for d in (2, 1, 3)]
    for cp in a5:
        cp.wait_recv()
    ta = s3a[x]
    for d in range(3):
        ta += r3[d, 0:56]
    for cp in b5:
        cp.wait_recv()
    tb = s3b[y]
    for d in range(3):
        tb += r3[d, 56:104]
    done = jnp.concatenate([ta, tb, jnp.zeros((8, 128), F32)], axis=0).astype(BF)
    out[c, z, y, x] = done
    T = (pl.ds(0, 64), pl.ds(64, 48))
    q = out.at[c, z, y, x]
    g1 = [send(q, q, p) for p in ZP]
    for cp in g1:
        cp.wait_recv()
    w0, w1 = out.at[c, :, y, x, T[0]], out.at[c, :, y, x, T[1]]
    g2 = [[send(q, q, p) for p in Q] for q, Q in ((w0, XP), (w1, YP))]
    w0, w1 = out.at[c, :, y, :, T[0]], out.at[c, :, :, x, T[1]]
    g3, last = [], []
    for i, (q, Q) in enumerate(((w0, YP), (w1, XP))):
        for cp in g2[i]:
            cp.wait_recv()
        g3.append([send(q, q, Q[d]) for d in (1, 0, 2)])
        last.append(send(q, q, CP))

    for i in range(3):
        arrived(st3[i])
    unit = (lax.rem(lane // 32, 2) == 0) == (c == 0)
    final = []
    for zz in range(4):

        def part(xi, carry):
            for q in range(2):
                a, b = xx[zz, xi, 2 * q], xx[zz, xi, 2 * q + 1]
                at = pl.ds(pl.multiple_of(zz * 1024 + xi * 256 + q * 128, 128), 128)
                recv[c, :, at] = jnp.where(unit, a, b)
                px[:, at] = jnp.where(unit, b, a)
            return carry

        lax.fori_loop(0, 4, part, 0)
        span = pl.ds(zz * 1024, 1024)
        final.append(send(px.at[:, span], recv.at[c, :, span], CP))

    for j, d in ((1, 1), (2, 3), (0, 2)):
        for i in range(2):
            g3[i][j].wait_recv()
            if i == 0:
                q = out.at[c, :, ys[4 - d], :, T[0]]
            else:
                q = out.at[c, :, :, xs[4 - d], T[1]]
            last.append(send(q, q, CP))
    for cp in last + final:
        cp.wait_recv()
    for cp in sent:
        cp.wait_send()


def exchange(rows, rel, bpart, pos, orow, grads):
    sem = pltpu.SemaphoreType.DMA
    v = pltpu.VMEM
    big = (4, 4, 4, HALF, 128)
    return pl.pallas_call(
        exchange_kernel,
        out_shape=(
            jax.ShapeDtypeStruct((2, 4, 4, 4, 112, 128), BF),
            jax.ShapeDtypeStruct((2, HALF, 4096), BF),
        ),
        in_specs=[VM] * 6,
        out_specs=(VM, VM),
        scratch_shapes=[
            v((8, 224, TRIP), BF), v((8, 1, TRIP), jnp.int32), v((8, 56, 128), F32), v((8, 104, 256), F32),
            v((4, 4, 104, 128), F32), v((3, 4, 56, 128), F32), v((3, 4, 48, 128), F32),
            v((4, 56, 128), F32), v((4, 48, 128), F32), v((3, 104, 128), F32),
            v((2 * HALF, 2 * TRIP), BF), v((256, 2 * TRIP), BF), v((2, 16, HALF, 256), BF), v((16, HALF, 256), BF),
            v(big, BF), v(big, BF), v(big, BF), v(big, BF), v((HALF, 4096), BF),
            sem((160,)), sem((160,)), sem((16,)),
        ],
        compiler_params=pltpu.CompilerParams(collective_id=1, has_side_effects=True, vmem_limit_bytes=56 * 2**20),
        cost_estimate=pl.CostEstimate(flops=8 * 10**10, bytes_accessed=10**7, transcendentals=0),
        name="exchange",
    )(rows, rel, bpart, pos, orow, grads)


def unpack_kernel(tiles, coef_out, bases_out):
    r = pl.program_id(0)
    z, c = r // 2, r % 2
    for q in range(15):
        coef_out[:, q * 128 : (q + 1) * 128] = tiles[c, z, q // 4, q % 4, 0:NB].astype(F32)

    @pl.when(r == 0)
    def _():
        for j in range(8):
            n = min(56, D - 56 * j)
            if n > 0:
                bases_out[56 * j : 56 * j + n, :] = tiles[j % 2, j // 2, 3, 3, 0:n, 0:NB].astype(F32)


def unpack(tiles):
    return pl.pallas_call(
        unpack_kernel,
        grid=(8,),
        out_shape=(jax.ShapeDtypeStruct((NB, NREL), F32), jax.ShapeDtypeStruct((D, NB), F32)),
        in_specs=[pl.BlockSpec((2, 4, 4, 4, 112, 128), lambda i: (0,) * 6)],
        out_specs=(pl.BlockSpec((NB, RANGE), lambda i: (0, i)), pl.BlockSpec((D, NB), lambda i: (0, 0))),
        compiler_params=pltpu.CompilerParams(vmem_limit_bytes=40 * 2**20),
        name="unpack",
    )(tiles)


def per_device(head_emb, tail_emb, relation, owners, owner_rows, entities, neg_rows, coef, bases):
    rel = relation.reshape(1, TRIP)
    own_neg, grads, rows, bases_part, pos = score(
        head_emb.T, tail_emb.T, rel, owners.T, neg_rows, bases.T, coef.T, entities.T
    )
    tiles, recv = exchange(rows, rel, bases_part, pos, owner_rows.T, grads)
    coef_grad, bases_grad = unpack(tiles)
    ent_grad = place(recv, own_neg, neg_rows)
    return ent_grad.T, coef_grad.T, bases_grad.T


def solution(mesh):
    rows = P(("grp", "dev"), None)
    return jax.shard_map(
        per_device,
        mesh=mesh,
        in_specs=(rows, rows, P(("grp", "dev")), rows, rows, rows, P(None, ("grp", "dev")), P(), P()),
        out_specs=(rows, P(), P()),
        check_vma=False,
    )
```

```python
import functools

import jax
import jax.numpy as jnp
from jax import lax
from jax.experimental import pallas as pl
from jax.experimental.pallas import tpu as pltpu
from jax.sharding import PartitionSpec as P

MESH = pl.DeviceIdType.MESH
HIGHEST = lax.Precision.HIGHEST
D = 400
NB = 100
TRIP = 1024
NEG = 128
ENT = 4096
NREL = 14824
GROUP = 32
NEG_ALL = NEG * GROUP
RA = (0, 208)
RB = (208, 192)
LOROW = 112
VM = pl.BlockSpec(memory_space=pltpu.VMEM)
ANY = pl.BlockSpec(memory_space=pl.ANY)
BF = jnp.bfloat16
F32 = jnp.float32


def dot(a, b, ca=1, cb=0, precision=None):
    return lax.dot_general(
        a, b, (((ca,), (cb,)), ((), ())), preferred_element_type=F32, precision=precision
    )


def spread(ids, rows):
    return (lax.broadcasted_iota(jnp.int32, (rows, ids.shape[1]), 0) == ids).astype(F32).astype(BF)


def equals(ids, value):
    return (ids == value).astype(F32).astype(BF)


def score_kernel(
    head, tail, rel, owners, negr, basest, coeft, entt,
    own_neg, grads, rows, bases_part, pos,
    coefv, entv, st, oh, pk, picked, relv, hrt, hr, mix, got, grd, pair, r2a, r2b, s3a, s3b, r3, blk,
    ss, rs, loc,
):
    g, k = lax.axis_index("grp"), lax.axis_index("dev")
    x, y, c = k // 8, lax.rem(k // 2, 4), lax.rem(k, 2)

    def dev(dx, dy, dc):
        return (g, (lax.rem(x + dx, 4) * 4 + lax.rem(y + dy, 4)) * 2 + lax.rem(c + dc, 2))

    get_ent = pltpu.make_async_copy(entt, entv, loc.at[0])
    get_ent.start()
    get_coef = pltpu.make_async_copy(coeft, coefv, loc.at[1])
    get_coef.start()
    bar = pltpu.get_barrier_semaphore()
    XP = [dev(d, 0, 0) for d in (1, 2, 3)]
    YP = [dev(0, d, 0) for d in (1, 2, 3)]
    CP = dev(0, 0, 1)
    for p in XP + YP + [CP]:
        pl.semaphore_signal(bar, inc=1, device_id=p, device_id_type=MESH)
    count = [0]
    sent = []

    def send(src, dst, p):
        i = count[0]
        count[0] += 1
        cp = pltpu.make_async_remote_copy(
            src_ref=src, dst_ref=dst, send_sem=ss.at[i], recv_sem=rs.at[i], device_id=p, device_id_type=MESH
        )
        cp.start()
        sent.append(cp)
        return cp

    pick_neg = spread(negr[...], ENT)
    get_ent.wait()
    got[c, y, x] = dot(entv[...], pick_neg).astype(BF)
    pl.semaphore_wait(bar, 7)
    A, B = pl.ds(*RA), pl.ds(*RB)
    mine_a, mine_b = got.at[c, y, x, A], got.at[c, y, x, B]
    a1 = [send(mine_a, mine_a, XP[d]) for d in (1, 0, 2)]
    b1 = [send(mine_b, mine_b, YP[d]) for d in (1, 0, 2)]

    st[...] = jnp.zeros_like(st)
    pk[...] = jnp.zeros_like(pk)
    ids = rel[...]
    low = spread(ids & 255, 256)
    high = lax.shift_right_logical(ids, 8)
    get_coef.wait()

    def load_coef(base, width, at):
        part = coefv[:, pl.ds(base, width)]
        first = part.astype(BF)
        st[0:NB, at : at + width] = first
        st[LOROW : LOROW + NB, at : at + width] = (part - first.astype(F32)).astype(BF)

    def gather(step):
        base = pl.multiple_of(step * 1024, 1024)
        load_coef(base, 1024, 0)
        for q in range(4):
            oh[q * 256 : (q + 1) * 256, :] = low * equals(high, step * 4 + q)
        pk[...] += dot(st[...], oh[...])

    def gather_loop(start, stop):
        def body(i, carry):
            gather(i)
            return carry

        lax.fori_loop(start, stop, body, 0)

    gather_loop(0, 5)
    for cp in a1:
        cp.wait_recv()
    line_a = got.at[c, y, :, A]
    a2 = [send(line_a, line_a, YP[d]) for d in (1, 0, 2)]
    for cp in b1:
        cp.wait_recv()
    line_b = got.at[c, :, x, B]
    b2 = [send(line_b, line_b, XP[d]) for d in (1, 0, 2)]
    last = [send(line_a, line_a, CP), send(line_b, line_b, CP)]

    gather_loop(5, 14)
    full = NREL // 1024 * 1024
    rest = NREL - full - 256
    load_coef(full, 256, 0)
    load_coef(full + 256, rest, 256)
    for q in range(2):
        oh[q * 256 : (q + 1) * 256, :] = low * equals(high, full // 256 + q)
    pk[...] += dot(st[:, 0 : 256 + rest], oh[0 : 256 + rest, :])
    chosen = pk[0:NB] + pk[LOROW : LOROW + NB]
    picked[...] = chosen
    relv[...] = dot(basest[...], chosen, precision=HIGHEST)
    hb = (head[...].astype(F32) * relv[...]).astype(BF)
    hrt[...] = hb
    hr[...] = hb.T
    tri = (
        lax.broadcasted_iota(jnp.int32, (256, 256), 0) < lax.broadcasted_iota(jnp.int32, (256, 256), 1)
    ).astype(F32).astype(BF)
    before = jnp.zeros((128, 1), F32)
    for h in range(2):
        for b in range(4):
            o = owners[h : h + 1, b * 256 : (b + 1) * 256]
            one = spread(o, 128)
            onef = one.astype(F32)
            rank = jnp.sum((dot(one, tri) + before) * onef, axis=0, keepdims=True)
            before = before + jnp.sum(onef, axis=1, keepdims=True)
            chip = lax.shift_right_logical(o, 1)
            pos[h : h + 1, b * 256 : (b + 1) * 256] = (
                lax.shift_right_logical(chip, 1) * 128
                + lax.rem((chip & 1) + c, 2) * 64
                + lax.rem((o & 1) + y, 2) * 32
                + rank.astype(jnp.int32)
            )

    for j, d in ((1, 1), (2, 3), (0, 2)):
        a2[j].wait_recv()
        r = got.at[c, lax.rem(y - d + 4, 4), :, A]
        last.append(send(r, r, CP))
        b2[j].wait_recv()
        r = got.at[c, :, lax.rem(x - d + 4, 4), B]
        last.append(send(r, r, CP))
    for cp in last:
        cp.wait_recv()

    mix[...] = jnp.zeros_like(mix)

    def chunk(cc, yy):
        for q in range(4):
            blk[:, q * 128 : (q + 1) * 128] = got[cc, yy, q]
        n = blk[...]
        s = dot(hr[...], n)
        prob = (0.5 * jnp.tanh(0.5 * s) + 0.5).astype(BF)
        mix[...] += dot(n, prob, 1, 1)
        part = (dot(hrt[...], prob) * (1.0 / NEG_ALL)).astype(BF)
        for q in range(4):
            grd[cc, yy, q] = part[:, q * 128 : (q + 1) * 128]

    halves = []
    for s in range(4):
        yy = lax.rem(y + 1 + s, 4)
        chunk(1 - c, yy)
        halves.append(send(grd.at[1 - c, yy], pair.at[yy], CP))
    a4, b4 = [], []
    for s in range(4):
        yy = lax.rem(y + 1 + s, 4)
        chunk(c, yy)
        halves[s].wait_recv()
        grd[c, yy] = (grd[c, yy].astype(F32) + pair[yy].astype(F32)).astype(BF)
        if s < 3:
            a4.append(send(grd.at[c, yy, :, A], r2a.at[s], YP[s]))
        for d in (1, 2, 3):
            xx = lax.rem(x + d, 4)
            b4.append(send(grd.at[c, yy, xx, B], r2b.at[d - 1, yy], XP[d - 1]))

    h, t = head[...].astype(F32), tail[...].astype(F32)
    rv = relv[...]
    hrv = h * rv
    score = jnp.sum(hrv * t, axis=0, keepdims=True)
    gate = 0.5 - 0.5 * jnp.tanh(0.5 * score)
    mean = mix[...] * (1.0 / NEG_ALL)
    inner = mean - gate * t
    grads[0] = (rv * inner).astype(BF)
    grads[1] = (-gate * hrv).astype(BF)
    rg = h * inner

    for cp in a4:
        cp.wait_recv()
    tot = grd[c, y, :, 0:208, :].astype(F32)
    for d in range(3):
        tot += r2a[d].astype(F32)
    s3a[...] = tot.astype(BF)
    a5 = [send(s3a.at[lax.rem(x + d, 4)], r3.at[d - 1, A], XP[d - 1]) for d in (1, 2, 3)]
    for cp in b4:
        cp.wait_recv()
    tot = grd[c, :, x, 208:400, :].astype(F32)
    for d in range(3):
        tot += r2b[d].astype(F32)
    s3b[...] = tot.astype(BF)
    b5 = [send(s3b.at[lax.rem(y + d, 4)], r3.at[d - 1, B], YP[d - 1]) for d in (1, 2, 3)]

    crow = dot(basest[...], rg, 0, 0, precision=HIGHEST)
    first = crow.astype(BF)
    rows[...] = jnp.zeros_like(rows)
    rows[0:NB] = first
    rows[LOROW : LOROW + NB] = (crow - first.astype(F32)).astype(BF)
    bases_part[...] = jnp.zeros_like(bases_part)
    bases_part[0:D, 0:NB] = dot(rg, picked[...], 1, 1, precision=HIGHEST)

    for cp in a5:
        cp.wait_recv()
    tot = s3a[x].astype(F32)
    for d in range(3):
        tot += r3[d, 0:208].astype(F32)
    own_neg[0:208] = tot
    for cp in b5:
        cp.wait_recv()
    tot = s3b[y].astype(F32)
    for d in range(3):
        tot += r3[d, 208:400].astype(F32)
    own_neg[208:400] = tot
    for cp in sent:
        cp.wait_send()


def score(head, tail, rel, owners, negr, basest, coeft, entt):
    sem = pltpu.SemaphoreType.DMA
    v = pltpu.VMEM
    return pl.pallas_call(
        score_kernel,
        out_shape=(
            jax.ShapeDtypeStruct((D, NEG), F32),
            jax.ShapeDtypeStruct((2, D, TRIP), BF),
            jax.ShapeDtypeStruct((224, TRIP), BF),
            jax.ShapeDtypeStruct((448, 128), F32),
            jax.ShapeDtypeStruct((2, TRIP), jnp.int32),
        ),
        in_specs=[VM] * 6 + [ANY] * 2,
        out_specs=(VM,) * 5,
        scratch_shapes=[
            v((NB, NREL), F32), v((D, ENT), BF), v((224, 1024), BF), v((1024, TRIP), BF), v((224, TRIP), F32),
            v((NB, TRIP), F32), v((D, TRIP), F32), v((D, TRIP), BF), v((TRIP, D), BF), v((D, TRIP), F32),
            v((2, 4, 4, D, NEG), BF), v((2, 4, 4, D, NEG), BF), v((4, 4, D, NEG), BF),
            v((3, 4, 208, NEG), BF), v((3, 4, 192, NEG), BF), v((4, 208, NEG), BF), v((4, 192, NEG), BF),
            v((3, D, NEG), BF), v((D, 512), BF),
            sem((48,)), sem((48,)), sem((2,)),
        ],
        compiler_params=pltpu.CompilerParams(collective_id=0, has_side_effects=True, vmem_limit_bytes=56 * 2**20),
        cost_estimate=pl.CostEstimate(flops=10**11, bytes_accessed=10**7, transcendentals=4 * 10**6),
        name="score",
    )(head, tail, rel, owners, negr, basest, coeft, entt)


WIDE = 4096 + 2 * NEG
HALF = 208


def place_kernel(recv, own_neg, negr, out, rt, low, ids):
    step = pl.program_id(0)

    @pl.when(step == 0)
    def _():
        rt[0:HALF, 0:4096] = recv[0]
        rt[HALF:D, 0:4096] = recv[1, 0 : D - HALF]
        a = recv[1, D - HALF : HALF].astype(F32)
        ids[:, 0:4096] = (a[0:1] * 64.0 + a[1:2]).astype(jnp.int32)
        n = own_neg[...]
        first = n.astype(BF)
        rt[0:D, 4096 : 4096 + NEG] = first
        rt[0:D, 4096 + NEG : WIDE] = (n - first.astype(F32)).astype(BF)
        ids[:, 4096 : 4096 + NEG] = negr[...]
        ids[:, 4096 + NEG : WIDE] = negr[...]
        for q in range(WIDE // 256):
            at = q * 256
            low[at : at + 256, :] = spread(ids[:, at : at + 256] & 255, 256).T

    for q in range(2):
        keep = equals(lax.shift_right_logical(ids[...], 8), step * 2 + q)
        out[:, q * 256 : (q + 1) * 256] = dot(rt[...] * keep, low[...])


def place(recv, own_neg, negr):
    whole = lambda *s: pl.BlockSpec(s, lambda i: (0,) * len(s))
    return pl.pallas_call(
        place_kernel,
        grid=(8,),
        out_shape=jax.ShapeDtypeStruct((D, ENT), F32),
        in_specs=[whole(2, HALF, 4096), whole(D, NEG), whole(1, NEG)],
        out_specs=pl.BlockSpec((D, 512), lambda i: (0, i)),
        scratch_shapes=[pltpu.VMEM((D, WIDE), BF), pltpu.VMEM((WIDE, 256), BF), pltpu.VMEM((1, WIDE), jnp.int32)],
        compiler_params=pltpu.CompilerParams(vmem_limit_bytes=40 * 2**20),
        cost_estimate=pl.CostEstimate(flops=14 * 10**9, bytes_accessed=11 * 10**6, transcendentals=0),
        name="place",
    )(recv, own_neg, negr)


RANGE = 1920


def exchange_kernel(
    rows, rel, bpart, pos, orow, grads, out, recv,
    gr, gi, gb, acc, rsb, r2a, r2b, s3a, s3b, r3,
    gx, low, pk, pb, w, v, u, xx, px, ss, rs, loc,
):
    z, k = lax.axis_index("grp"), lax.axis_index("dev")
    x, y, c = k // 8, lax.rem(k // 2, 4), lax.rem(k, 2)
    own = z * 2 + c

    def dev(dx, dy, dz, dc):
        return (lax.rem(z + dz, 4), (lax.rem(x + dx, 4) * 4 + lax.rem(y + dy, 4)) * 2 + lax.rem(c + dc, 2))

    XP = [dev(d, 0, 0, 0) for d in (1, 2, 3)]
    YP = [dev(0, d, 0, 0) for d in (1, 2, 3)]
    ZP = [dev(0, 0, d, 0) for d in (1, 2, 3)]
    ZC = [dev(0, 0, d, 1) for d in (1, 2, 3)]
    CP = dev(0, 0, 0, 1)
    xs = [lax.rem(x + d, 4) for d in range(4)]
    ys = [lax.rem(y + d, 4) for d in range(4)]
    zs = [lax.rem(z + d, 4) for d in range(4)]
    bar = pltpu.get_barrier_semaphore()
    for p in XP + YP + ZP + ZC + [CP]:
        pl.semaphore_signal(bar, inc=1, device_id=p, device_id_type=MESH)
    local = []

    def keep(src, dst):
        cp = pltpu.make_async_copy(src, dst, loc.at[len(local)])
        cp.start()
        local.append(cp)
        return cp

    kept = [
        keep(rows, gr.at[own]),
        keep(rel, gi.at[own]),
        keep(bpart.at[pl.ds(pl.multiple_of(own * 56, 8), 56)], gb.at[own]),
    ]
    count = [16]
    sent = []

    def remote(src, dst, i, p):
        return pltpu.make_async_remote_copy(
            src_ref=src, dst_ref=dst, send_sem=ss.at[i], recv_sem=rs.at[i], device_id=p, device_id_type=MESH
        )

    def send(src, dst, p):
        cp = remote(src, dst, count[0], p)
        count[0] += 1
        cp.start()
        sent.append(cp)
        return cp

    for h in range(2):
        at = h * TRIP
        low[:, at : at + TRIP] = spread(pos[h : h + 1] & 255, 256)
        r = orow[h : h + 1]
        two = lax.broadcasted_iota(jnp.int32, (16, TRIP), 0)
        extra = jnp.where(two == 0, lax.shift_right_logical(r, 6), jnp.where(two == 1, r & 63, 0))
        gx[0:D, at : at + TRIP] = grads[h]
        gx[D : D + 16, at : at + TRIP] = extra.astype(F32).astype(BF)
    for cp in kept:
        cp.wait()
    pl.semaphore_wait(bar, 13)
    first = [[send(rel, gi.at[own], p), send(rows, gr.at[own], p)] for p in (ZP[0], ZP[2])]
    zm, zp = zs[3] * 2 + c, zs[1] * 2 + c
    HI, LO = pl.ds(0, LOROW), pl.ds(LOROW, LOROW)

    def pass_on():
        for cp in first[0]:
            cp.wait_recv()
        away = [send(gi.at[zm], gi.at[zm], ZP[0]), send(gr.at[zm, HI], gr.at[zm, HI], ZP[0])]
        for cp in first[1]:
            cp.wait_recv()
        return away + [send(gr.at[zp, LO], gr.at[zp, LO], ZP[2])]

    near = [send(rel, gi.at[own], CP), send(rows, gr.at[own], CP)]
    pieces = []

    def piece(dz, dc, p):
        r = zs[dz] * 2 + lax.rem(c + dc, 2)
        pieces.append(send(bpart.at[pl.ds(pl.multiple_of(r * 56, 8), 56)], gb.at[own], p))

    piece(0, 1, CP)
    for d in (1, 2, 3):
        piece(d, 0, ZP[d - 1])
        piece(d, 1, ZC[d - 1])

    S = (pl.ds(0, 80), pl.ds(80, 64), pl.ds(144, 64))
    high = [lax.shift_right_logical(pos[h : h + 1], 8) for h in range(2)]
    lane = lax.broadcasted_iota(jnp.int32, (HALF, 128), 1)
    side = (lane // 64) == c
    st1 = [[], [], []]

    def swap(s):
        return remote(pk.at[1 - c, s], pb.at[s], s, CP)

    for gp in range(4):
        zz = zs[(gp + 1) % 4]

        def fill(j, carry):
            s = zz * 4 + j
            tot = None
            for h in range(2):
                at = h * TRIP
                one = low[:, at : at + TRIP] * equals(high[h], s)
                d = dot(gx[:, at : at + TRIP], one, 1, 1)
                tot = d if tot is None else tot + d
            pk[0, s] = tot[0:HALF].astype(BF)
            pk[1, s] = tot[HALF : 2 * HALF].astype(BF)
            swap(s).start()
            return carry

        def join(j, carry):
            s = zz * 4 + j
            swap(s).wait()
            for q in range(2):
                a = pk[c, s, :, q * 128 : (q + 1) * 128]
                b = pb[s, :, q * 128 : (q + 1) * 128]
                w[zz, j, 2 * q] = jnp.where(side, a, b)
                w[zz, j, 2 * q + 1] = jnp.where(side, b, a)
            return carry

        lax.fori_loop(0, 4, fill, 0)
        lax.fori_loop(0, 4, join, 0)
        for d in (1, 3, 2):
            st1[0].append(send(w.at[zz, xs[d], :, S[0]], v.at[zz, x, :, S[0]], XP[d - 1]))
            st1[1].append(send(w.at[zz, :, ys[d], S[1]], v.at[zz, :, y, S[1]], YP[d - 1]))
        if gp == 2:
            away = pass_on()
        if gp < 3:
            st1[2].append(send(w.at[zz, :, :, S[2]], v.at[z, :, :, S[2]], ZP[gp]))
    st1[0].append(keep(w.at[:, x, :, S[0]], v.at[:, x, :, S[0]]))
    st1[1].append(keep(w.at[:, :, y, S[1]], v.at[:, :, y, S[1]]))
    st1[2].append(keep(w.at[z, :, :, S[2]], v.at[z, :, :, S[2]]))

    def arrived(cps):
        for cp in cps[:-1]:
            cp.wait_recv()
        cps[-1].wait()

    def along_x(a, b, s):
        cps = [send(a.at[:, xs[d], :, s], b.at[:, x, :, s], XP[d - 1]) for d in (1, 3, 2)]
        return cps + [keep(a.at[:, x, :, s], b.at[:, x, :, s])]

    def along_y(a, b, s):
        cps = [send(a.at[:, :, ys[d], s], b.at[:, :, y, s], YP[d - 1]) for d in (1, 3, 2)]
        return cps + [keep(a.at[:, :, y, s], b.at[:, :, y, s])]

    def along_z(a, b, s):
        cps = [send(a.at[zs[d], :, :, s], b.at[z, :, :, s], ZP[d - 1]) for d in (1, 3, 2)]
        return cps + [keep(a.at[z, :, :, s], b.at[z, :, :, s])]

    def add(j, start):
        ids = gi[j] - own * RANGE
        lo = spread(ids & 255, 256)
        hi = lax.shift_right_arithmetic(ids, 8)
        r = gr[j]
        for t in range(8):
            p = dot(r * equals(hi, t), lo, 1, 1)
            p = p[0:104] + p[LOROW : LOROW + 104]
            if start:
                acc[t] = p
            else:
                acc[t] += p

    add(own, True)
    for cp in near:
        cp.wait_recv()
    add(z * 2 + 1 - c, False)

    st2 = []
    for i, go in enumerate((along_y, along_z, along_x)):
        arrived(st1[i])
        st2.append(go(v, u, S[i]))

    for i, d in enumerate((1, 3, 2)):
        from_z = zs[4 - d] * 2
        if i == 2:
            for cp in away:
                cp.wait_recv()
        more = [send(gi.at[from_z + c], gi.at[from_z + c], CP), send(gr.at[from_z + c], gr.at[from_z + c], CP)]
        add(from_z + c, False)
        for cp in more:
            cp.wait_recv()
        add(from_z + 1 - c, False)
    for cp in pieces:
        cp.wait_recv()
    tot = gb[0]
    for j in range(1, 8):
        tot += gb[j]
    for q in range(16):
        if q == 15:
            rsb[3, 3] = jnp.zeros((104, 128), F32)
            rsb[3, 3, 0:56] = tot
        else:
            rsb[q // 4, q % 4] = acc[q // 2, :, (q % 2) * 128 : (q % 2) * 128 + 128]

    A, B = pl.ds(0, 56), pl.ds(56, 48)
    a4, b4 = [], []
    for d in (2, 1, 3):
        a4.append(send(rsb.at[ys[d], :, A], r2a.at[d - 1], YP[d - 1]))
        b4.append(send(rsb.at[:, xs[d], B], r2b.at[d - 1], XP[d - 1]))
    st3 = []
    for i, go in enumerate((along_z, along_x, along_y)):
        arrived(st2[i])
        st3.append(go(u, xx, S[i]))

    for cp in a4:
        cp.wait_recv()
    t4 = rsb[y, :, 0:56, :]
    for d in range(3):
        t4 += r2a[d]
    s3a[...] = t4
    a5 = [send(s3a.at[xs[d]], r3.at[d - 1, A], XP[d - 1]) for d in (2, 1, 3)]
    for cp in b4:
        cp.wait_recv()
    t4 = rsb[:, x, 56:104, :]
    for d in range(3):
        t4 += r2b[d]
    s3b[...] = t4
    b5 = [send(s3b.at[ys[d]], r3.at[d - 1, B], YP[d - 1]) for d in (2, 1, 3)]
    for cp in a5:
        cp.wait_recv()
    ta = s3a[x]
    for d in range(3):
        ta += r3[d, 0:56]
    for cp in b5:
        cp.wait_recv()
    tb = s3b[y]
    for d in range(3):
        tb += r3[d, 56:104]
    done = jnp.concatenate([ta, tb, jnp.zeros((8, 128), F32)], axis=0).astype(BF)
    out[c, z, y, x] = done
    T = (pl.ds(0, 64), pl.ds(64, 48))
    q = out.at[c, z, y, x]
    g1 = [send(q, q, p) for p in ZP]
    for cp in g1:
        cp.wait_recv()
    w0, w1 = out.at[c, :, y, x, T[0]], out.at[c, :, y, x, T[1]]
    g2 = [[send(q, q, p) for p in Q] for q, Q in ((w0, XP), (w1, YP))]
    w0, w1 = out.at[c, :, y, :, T[0]], out.at[c, :, :, x, T[1]]
    g3, last = [], []
    for i, (q, Q) in enumerate(((w0, YP), (w1, XP))):
        for cp in g2[i]:
            cp.wait_recv()
        g3.append([send(q, q, Q[d]) for d in (1, 0, 2)])
        last.append(send(q, q, CP))

    for i in range(3):
        arrived(st3[i])
    unit = (lax.rem(lane // 32, 2) == 0) == (c == 0)
    final = []
    for zz in range(4):

        def part(xi, carry):
            for q in range(2):
                a, b = xx[zz, xi, 2 * q], xx[zz, xi, 2 * q + 1]
                at = pl.ds(pl.multiple_of(zz * 1024 + xi * 256 + q * 128, 128), 128)
                recv[c, :, at] = jnp.where(unit, a, b)
                px[:, at] = jnp.where(unit, b, a)
            return carry

        lax.fori_loop(0, 4, part, 0)
        span = pl.ds(zz * 1024, 1024)
        final.append(send(px.at[:, span], recv.at[c, :, span], CP))

    for j, d in ((1, 1), (2, 3), (0, 2)):
        for i in range(2):
            g3[i][j].wait_recv()
            if i == 0:
                q = out.at[c, :, ys[4 - d], :, T[0]]
            else:
                q = out.at[c, :, :, xs[4 - d], T[1]]
            last.append(send(q, q, CP))
    for cp in last + final:
        cp.wait_recv()
    for cp in sent:
        cp.wait_send()


def exchange(rows, rel, bpart, pos, orow, grads):
    sem = pltpu.SemaphoreType.DMA
    v = pltpu.VMEM
    big = (4, 4, 4, HALF, 128)
    return pl.pallas_call(
        exchange_kernel,
        out_shape=(
            jax.ShapeDtypeStruct((2, 4, 4, 4, 112, 128), BF),
            jax.ShapeDtypeStruct((2, HALF, 4096), BF),
        ),
        in_specs=[VM] * 6,
        out_specs=(VM, VM),
        scratch_shapes=[
            v((8, 224, TRIP), BF), v((8, 1, TRIP), jnp.int32), v((8, 56, 128), F32), v((8, 104, 256), F32),
            v((4, 4, 104, 128), F32), v((3, 4, 56, 128), F32), v((3, 4, 48, 128), F32),
            v((4, 56, 128), F32), v((4, 48, 128), F32), v((3, 104, 128), F32),
            v((2 * HALF, 2 * TRIP), BF), v((256, 2 * TRIP), BF), v((2, 16, HALF, 256), BF), v((16, HALF, 256), BF),
            v(big, BF), v(big, BF), v(big, BF), v(big, BF), v((HALF, 4096), BF),
            sem((160,)), sem((160,)), sem((16,)),
        ],
        compiler_params=pltpu.CompilerParams(collective_id=1, has_side_effects=True, vmem_limit_bytes=56 * 2**20),
        cost_estimate=pl.CostEstimate(flops=8 * 10**10, bytes_accessed=10**7, transcendentals=0),
        name="exchange",
    )(rows, rel, bpart, pos, orow, grads)


def unpack_kernel(tiles, coef_out, bases_out):
    r = pl.program_id(0)
    z, c = r // 2, r % 2
    for q in range(15):
        coef_out[:, q * 128 : (q + 1) * 128] = tiles[c, z, q // 4, q % 4, 0:NB].astype(F32)

    @pl.when(r == 0)
    def _():
        for j in range(8):
            n = min(56, D - 56 * j)
            if n > 0:
                bases_out[56 * j : 56 * j + n, :] = tiles[j % 2, j // 2, 3, 3, 0:n, 0:NB].astype(F32)


def unpack(tiles):
    return pl.pallas_call(
        unpack_kernel,
        grid=(8,),
        out_shape=(jax.ShapeDtypeStruct((NB, NREL), F32), jax.ShapeDtypeStruct((D, NB), F32)),
        in_specs=[pl.BlockSpec((2, 4, 4, 4, 112, 128), lambda i: (0,) * 6)],
        out_specs=(pl.BlockSpec((NB, RANGE), lambda i: (0, i)), pl.BlockSpec((D, NB), lambda i: (0, 0))),
        compiler_params=pltpu.CompilerParams(vmem_limit_bytes=40 * 2**20),
        name="unpack",
    )(tiles)


def per_device(head_emb, tail_emb, relation, owners, owner_rows, entities, neg_rows, coef, bases):
    rel = relation.reshape(1, TRIP)
    own_neg, grads, rows, bases_part, pos = score(
        head_emb.T, tail_emb.T, rel, owners.T, neg_rows, bases.T, coef.T, entities.T
    )
    tiles, recv = exchange(rows, rel, bases_part, pos, owner_rows.T, grads)
    coef_grad, bases_grad = unpack(tiles)
    ent_grad = place(recv, own_neg, neg_rows)
    return ent_grad.T, coef_grad.T, bases_grad.T


def solution(mesh):
    rows = P(("grp", "dev"), None)
    return jax.shard_map(
        per_device,
        mesh=mesh,
        in_specs=(rows, rows, P(("grp", "dev")), rows, rows, rows, P(None, ("grp", "dev")), P(), P()),
        out_specs=(rows, P(), P()),
        check_vma=False,
    )
```
